512 devices in a mesh: pts: 32 (over z_hi, y, core), val: 16 (over z_lo, x).
Axes of the slice: x: 4, y: 8, z: 8 (z_hi: 2, z_lo: 4; z = z_hi * 4 + z_lo), core: 2. Of those that a mesh axis runs over, the one named last changes fastest.
Arguments:
- vectors: float32 [1, 512, 2048], P(None, 'val', 'pts'), may hold values from -6 to 6
- eval_energy: float32 [512], P('val'), may hold values from -2 to -0.2
- cond_energy: float32 [2048], P('pts'), may hold values from 0.2 to 2
- val_orbitals: float32 [512, 8192], P('pts', 'val'), may hold values from -0.25 to 0.25
- cond_orbitals: float32 [2048, 8192], P('val', 'pts'), may hold values from -0.125 to 0.125
- screened: float32 [8192, 8192], P('val', 'pts'), may hold values from -1.5 to 1.5
Outputs:
- filtered: float32 [1, 512, 2048], P(None, 'val', 'pts')
The draws below stay inside these ranges and needn't reach their ends.
All inputs are finite; a program needn't handle non-finite values.
Results may differ from the reference program's by a relative error of at most 0.00013.
Values sent between devices are 32-bit elements; how exact they have to be, the bound alone decides.
No kernel may reach another device: no remote copies, remote signals or barrier semaphores. Data moves between devices by JAX's collectives and lax.ppermute only.
A program may use at most 64 MiB of HBM per device.

```python
import jax
import jax.numpy as jnp
from jax import lax

NV = 512
NC = 2048
NP = 8192
BATCH = 1
ITERS = 2


def block_levels(own_key, dims, pieces, low, top_value):
    def one(axis_at, parts):
        heights = jax.random.uniform(jax.random.fold_in(jax.random.fold_in(own_key, 6), axis_at), (parts,), jnp.float32, low / len(pieces), top_value / len(pieces))
        return jnp.repeat(jnp.exp(heights), dims[axis_at] // parts).reshape((-1,) + (1,) * (len(dims) - axis_at - 1))

    level = one(*pieces[0])
    for cut in pieces[1:]:
        level = level * one(*cut)
    return level


def scatter_about(stream_key, dims, spread, bound, cuts=(), dtype=jnp.bfloat16):
    loudness = block_levels(stream_key, dims, cuts, -0.22, 0.18) if cuts else 1.0
    array = jax.random.normal(stream_key, dims, jnp.float32) * spread * loudness
    return jnp.minimum(jnp.maximum(array, -bound), bound).astype(dtype)


def setup_inputs(seed: int = 0) -> dict:
    key_list = jax.random.split(jax.random.key(seed), 7)
    vectors = scatter_about(key_list[0], (BATCH, NV, NC), 1.0, 6.0, ((1, 16), (2, 32)), jnp.float32)
    eval_energy = jnp.clip(-2.0 + 1.8 * jax.random.uniform(key_list[1], (NV,), jnp.float32) ** block_levels(key_list[1], (NV,), ((0, 16),), -0.2, 0.2), -2.0, -0.2)
    cond_energy = jnp.clip(0.2 + 1.8 * jax.random.uniform(key_list[2], (NC,), jnp.float32) ** block_levels(key_list[2], (NC,), ((0, 32),), -0.2, 0.2), 0.2, 2.0)
    val_orbitals = scatter_about(key_list[3], (NV, NP), NV ** -0.5, 0.25, ((0, 32), (1, 16)), jnp.float32)
    cond_orbitals = scatter_about(key_list[4], (NC, NP), NC ** -0.5, 0.125, ((0, 16), (1, 32)), jnp.float32)
    screened = scatter_about(key_list[5], (NP, NP), (NP * NP // (4 * NV * NC)) ** -0.5, 1.5, ((0, 16), (1, 32)), jnp.float32)
    return dict(vectors=vectors, eval_energy=eval_energy, cond_energy=cond_energy, val_orbitals=val_orbitals, cond_orbitals=cond_orbitals, screened=screened)


CENTER = 2.2
HALF_WIDTH = 2.0


def apply_direct(vec, val_orbitals, cond_orbitals, screened):
    highest = lax.Precision.HIGHEST

    def single(x):
        pair = jnp.dot(x, cond_orbitals, precision=highest, preferred_element_type=jnp.float32)
        mixed = jnp.dot(val_orbitals.T, pair, precision=highest, preferred_element_type=jnp.float32)
        weighted = mixed * screened
        back = jnp.dot(val_orbitals, weighted, precision=highest, preferred_element_type=jnp.float32)
        return jnp.dot(back, cond_orbitals.T, precision=highest, preferred_element_type=jnp.float32)

    return lax.map(single, vec)


def reference(vectors, eval_energy, cond_energy, val_orbitals, cond_orbitals, screened):
    ediff = cond_energy[None, None, :] - eval_energy[None, :, None]
    older = vectors
    newer = vectors
    for step in range(ITERS):
        hamil = ediff * newer - apply_direct(newer, val_orbitals, cond_orbitals, screened)
        scaled = (hamil - CENTER * newer) / HALF_WIDTH
        if step == 0:
            following = scaled
        else:
            following = 2.0 * scaled - older
        older = newer
        newer = following
    return newer
```

```python
import functools

import jax
import jax.numpy as jnp
from jax import lax
from jax.experimental import pallas as pl
from jax.experimental.pallas import tpu as pltpu
from jax.sharding import Mesh
from jax.sharding import PartitionSpec as P

ITERS = 2
CENTER = 2.2
HALF_WIDTH = 2.0

ROWS = ("zh", "y")
PTS = ("zh", "y", "core")
VAL = ("zl", "x")

F32 = jnp.float32
BF16 = jnp.bfloat16
PARAMS = pltpu.CompilerParams(vmem_limit_bytes=20 * 1024 * 1024)


def split(a):
    hi = a.astype(BF16)
    return hi, (a - hi.astype(F32)).astype(BF16)


def dot(a, b):
    return jnp.dot(a, b, preferred_element_type=F32)


def dot_nt(a, b):
    return lax.dot_general(a, b, (((1,), (1,)), ((), ())), preferred_element_type=F32)


def exchange(blocks, axes):
    return lax.all_to_all(blocks, axes, 0, 0, tiled=True)


def copied(array, axes):
    return exchange(jnp.broadcast_to(array[None], (lax.axis_size(axes), *array.shape)), axes)


def packed(block):
    half = block.shape[0] // 2
    return jnp.concatenate([block[:half], block[half:]], axis=1)


def join_pairs(gathered_ref, xh_ref, xl_ref, order):
    half, width = gathered_ref.shape[1:]
    left = lax.broadcasted_iota(jnp.int32, (half, width), 1) < width // 2
    for q, place in enumerate(order):
        a, b = gathered_ref[2 * q], gathered_ref[2 * q + 1]
        upper = jnp.where(left, a, pltpu.roll(b, width // 2, 1))
        lower = jnp.where(left, pltpu.roll(a, width // 2, 1), b)
        cols = slice(place * width, (place + 1) * width)
        for part, rows in ((upper, slice(0, half)), (lower, slice(half, 2 * half))):
            hi, lo = split(part)
            xh_ref[rows, cols] = hi
            xl_ref[rows, cols] = lo


def pair_first_kernel(order, gathered_ref, cond_ref, pair_ref, ch_ref, cl_ref, xh_ref, xl_ref):
    join_pairs(gathered_ref, xh_ref, xl_ref, order)
    ch, cl = split(cond_ref[...])
    ch_ref[...] = ch
    cl_ref[...] = cl
    pair = dot(xh_ref[...], ch) + (dot(xh_ref[...], cl) + dot(xl_ref[...], ch))
    pair_ref[...] = jnp.broadcast_to(pair[None], pair_ref.shape)


def pair_kernel(order, gathered_ref, ch_ref, cl_ref, pair_ref, xh_ref, xl_ref):
    join_pairs(gathered_ref, xh_ref, xl_ref, order)
    ch, cl = ch_ref[...], cl_ref[...]
    pair = dot(xh_ref[...], ch) + (dot(xh_ref[...], cl) + dot(xl_ref[...], ch))
    pair_ref[...] = jnp.broadcast_to(pair[None], pair_ref.shape)


def orbitals_kernel(val_ref, vh_ref, vl_ref, th_ref, tl_ref):
    cores, chips, depth, _ = val_ref.shape
    for chip in range(chips):
        for core in range(cores):
            at = (chip * cores + core) * depth
            hi, lo = split(val_ref[core, chip])
            vh_ref[at : at + depth, :] = hi
            vl_ref[at : at + depth, :] = lo
    whole = jnp.concatenate(
        [val_ref[core, chip] for chip in range(chips) for core in range(cores)], axis=0
    )
    hi, lo = split(whole.T)
    th_ref[...] = hi
    tl_ref[...] = lo


def screen_kernel(pair_ref, screened_ref, vh_ref, vl_ref, th_ref, tl_ref, back_ref):
    ph, pl_ = split(pair_ref[...])
    mixed = dot(th_ref[...], ph) + (dot(th_ref[...], pl_) + dot(tl_ref[...], ph))
    wh, wl = split(mixed * screened_ref[...])
    back_ref[...] = dot(vh_ref[...], wh) + (dot(vh_ref[...], wl) + dot(vl_ref[...], wh))


def direct_kernel(order, terms_ref, ch_ref, cl_ref, out_ref):
    bh, bl = split(jnp.sum(terms_ref[...], axis=0))
    ch, cl = ch_ref[...], cl_ref[...]
    direct = dot_nt(bh, ch) + (dot_nt(bl, ch) + dot_nt(bh, cl))
    half, width = out_ref.shape[1:]
    left = lax.broadcasted_iota(jnp.int32, (half, width), 1) < width // 2
    for q, place in enumerate(order):
        upper = direct[:half, place * width : (place + 1) * width]
        lower = direct[half:, place * width : (place + 1) * width]
        out_ref[2 * q] = jnp.where(left, upper, pltpu.roll(lower, width // 2, 1))
        out_ref[2 * q + 1] = jnp.where(left, pltpu.roll(upper, width // 2, 1), lower)


def scaled(terms_ref, vec, ediff_ref):
    hamil = ediff_ref[...] * vec - jnp.sum(terms_ref[...], axis=0)
    return (hamil - CENTER * vec) / HALF_WIDTH


def first_kernel(terms_ref, vec_ref, ediff_ref, new_ref, copies_ref):
    new = scaled(terms_ref, vec_ref[...], ediff_ref)
    new_ref[...] = new
    copies_ref[...] = jnp.broadcast_to(new[None], copies_ref.shape)


def last_kernel(terms_ref, vec_ref, older_ref, ediff_ref, out_ref):
    new = 2.0 * scaled(terms_ref, vec_ref[...], ediff_ref) - older_ref[...]
    half, width = new.shape
    out_ref[:half, :] = new[:, : width // 2]
    out_ref[half:, :] = new[:, width // 2 :]


def call(kernel, out_shapes, scratch=()):
    shapes = [jax.ShapeDtypeStruct(s, d) for s, d in out_shapes]
    return pl.pallas_call(
        kernel,
        out_shape=shapes if len(shapes) > 1 else shapes[0],
        scratch_shapes=[pltpu.VMEM(s, d) for s, d in scratch],
        compiler_params=PARAMS,
    )


def per_device(vectors, eval_energy, cond_energy, val_orbitals, cond_orbitals, screened):
    _, rows, cols = vectors.shape
    pts, val = lax.axis_size(PTS), lax.axis_size(VAL)
    nzl, nx = lax.axis_size("zl"), lax.axis_size("x")
    depth_c, points_c = cond_orbitals.shape
    depth_v, points_v = val_orbitals.shape
    nv, nc = rows * val, cols * pts
    half, width = rows // 2, cols * 2
    order = [x * nzl + zl for zl in range(nzl) for x in range(nx)]

    older = packed(vectors[0])
    ediff = packed(cond_energy[None, :] - eval_energy[:, None])

    cond_zl = copied(cond_orbitals, "zl")
    gathered = copied(older, PTS)
    val_chips = copied(val_orbitals, ROWS)
    cond_all = copied(cond_zl.reshape(nzl * depth_c, points_c), "x").reshape(nc, points_c)
    val_all = copied(val_chips, "core")
    vh, vl, th, tl = call(
        orbitals_kernel, [((nv, points_v), BF16)] * 2 + [((points_v, nv), BF16)] * 2
    )(val_all)

    newer = older
    for step in range(ITERS):
        scratch = [((rows, nc), BF16)] * 2
        if step == 0:
            pair, ch, cl = call(
                functools.partial(pair_first_kernel, order),
                [((val, rows, points_c), F32), ((nc, points_c), BF16), ((nc, points_c), BF16)],
                scratch,
            )(gathered, cond_all)
        else:
            pair = call(
                functools.partial(pair_kernel, order), [((val, rows, points_c), F32)], scratch
            )(gathered, ch, cl)
        pair_all = exchange(pair, VAL).reshape(nv, points_c)
        back = call(screen_kernel, [((nv, points_c), F32)])(pair_all, screened, vh, vl, th, tl)
        back = exchange(back.reshape(val, rows, points_c), VAL)
        direct = call(functools.partial(direct_kernel, order), [((pts, half, width), F32)])(
            back, ch, cl
        )
        direct = exchange(direct, PTS)
        if step < ITERS - 1:
            newer, copies = call(
                first_kernel, [((half, width), F32), ((pts, half, width), F32)]
            )(direct, older, ediff)
            gathered = exchange(copies, PTS)
    out = call(last_kernel, [((rows, cols), F32)])(direct, newer, older, ediff)
    return out[None]


def solution(mesh):
    torus = Mesh(mesh.devices.reshape(2, 8, 2, 4, 4), ("zh", "y", "core", "zl", "x"))
    placed = (P(None, VAL, PTS), P(VAL), P(PTS), P(PTS, VAL), P(VAL, PTS), P(VAL, PTS))
    return jax.shard_map(
        per_device, mesh=torus, in_specs=placed, out_specs=P(None, VAL, PTS), check_vma=False
    )
```

```python
import jax
import jax.numpy as jnp
from jax import lax
from jax.experimental import pallas as pl
from jax.experimental.pallas import tpu as pltpu
from jax.sharding import Mesh
from jax.sharding import PartitionSpec as P

ITERS = 2
CENTER = 2.2
HALF_WIDTH = 2.0

ROWS = ("zh", "y")
PTS = ("zh", "y", "core")
VAL = ("zl", "x")

NZ, NX = 4, 4
WIDTH = 128

F32 = jnp.float32
BF16 = jnp.bfloat16
PARAMS = pltpu.CompilerParams(vmem_limit_bytes=20 * 1024 * 1024)


def split(a):
    hi = a.astype(BF16)
    return hi, (a - hi.astype(F32)).astype(BF16)


def dot(a, b):
    return jnp.dot(a, b, preferred_element_type=F32)


def dot_nt(a, b):
    return lax.dot_general(a, b, (((1,), (1,)), ((), ())), preferred_element_type=F32)


def exchange(blocks, axes):
    return lax.all_to_all(blocks, axes, 0, 0, tiled=True)


def shifted(array, axis, by):
    n = lax.axis_size(axis)
    return lax.ppermute(array, axis, [(i, (i + by) % n) for i in range(n)])


def copied(array, axes):
    return exchange(jnp.broadcast_to(array[None], (lax.axis_size(axes), *array.shape)), axes)


def packed(block):
    half = block.shape[0] // 2
    return jnp.concatenate([block[:half], block[half:]], axis=1)


def place_pair(a, b, place, xh_ref, xl_ref):
    half, width = a.shape
    left = lax.broadcasted_iota(jnp.int32, (half, width), 1) < width // 2
    upper = jnp.where(left, a, pltpu.roll(b, width // 2, 1))
    lower = jnp.where(left, pltpu.roll(a, width // 2, 1), b)
    cols = slice(place * width, (place + 1) * width)
    for part, rows in ((upper, slice(0, half)), (lower, slice(half, 2 * half))):
        hi, lo = split(part)
        xh_ref[rows, cols] = hi
        xl_ref[rows, cols] = lo


def by_core(core, own, other):
    return jnp.where(core == 0, own, other), jnp.where(core == 0, other, own)


def begin_kernel(
    where_ref, own_hbm, other_hbm, ediff_ref, older_ref, mine_hbm, left_hbm, upper_hbm, lower_hbm, right_hbm,
    pair_ref, ch_ref, cl_ref, vh_ref, vl_ref, th_ref, tl_ref, ediff_out_ref, older_out_ref,
    own_ref, other_ref, cond_ref, xh_ref, xl_ref, sems,
):
    depth = mine_hbm.shape[0]
    part = upper_hbm.shape[0]
    copies = [
        pltpu.make_async_copy(own_hbm, own_ref, sems.at[0]),
        pltpu.make_async_copy(other_hbm, other_ref, sems.at[1]),
    ]
    at = 0
    for i, ref in enumerate((mine_hbm, left_hbm, upper_hbm, lower_hbm, right_hbm)):
        rows = ref.shape[0]
        copies.append(
            pltpu.make_async_copy(ref, cond_ref.at[pl.ds(at, rows)], sems.at[2 + i])
        )
        at += rows
    for copy in copies:
        copy.start()
    ediff_out_ref[...] = ediff_ref[...]
    older_out_ref[...] = older_ref[...]
    core = where_ref[NX * NZ]
    copies[0].wait()
    copies[1].wait()
    def slot_of(chip):
        return where_ref[NX * NZ + 1 + chip]

    for place in range(NX * NZ):
        q = slot_of(where_ref[place])
        own, other = own_ref[q][:, -WIDTH:], other_ref[q][:, -WIDTH:]
        place_pair(*by_core(core, own, other), place, xh_ref, xl_ref)
    points = vh_ref.shape[1]
    rows = []
    for chip in range(own_ref.shape[0]):
        q = slot_of(chip)
        rows.extend(by_core(core, own_ref[q][:, :points], other_ref[q][:, :points]))
    whole = jnp.concatenate(rows, axis=0)
    hi, lo = split(whole)
    vh_ref[...] = hi
    vl_ref[...] = lo
    hi, lo = split(whole.T)
    th_ref[...] = hi
    tl_ref[...] = lo
    for copy in copies[2:]:
        copy.wait()
    ch, cl = split(cond_ref[...])
    ch_ref[...] = ch
    cl_ref[...] = cl
    pair = dot(xh_ref[...], ch) + (dot(xh_ref[...], cl) + dot(xl_ref[...], ch))
    pair_ref[...] = jnp.broadcast_to(pair[None], pair_ref.shape)


def pair_kernel(where_ref, gathered_ref, ch_ref, cl_ref, pair_ref, xh_ref, xl_ref):
    for jx in range(NX):
        for jz in range(NZ):
            q = where_ref[jx * NZ + jz]
            place_pair(
                gathered_ref[2 * q], gathered_ref[2 * q + 1], jx * NZ + jz, xh_ref, xl_ref
            )
    ch, cl = ch_ref[...], cl_ref[...]
    pair = dot(xh_ref[...], ch) + (dot(xh_ref[...], cl) + dot(xl_ref[...], ch))
    pair_ref[...] = jnp.broadcast_to(pair[None], pair_ref.shape)


def screen_kernel(pair_ref, screened_ref, vh_ref, vl_ref, th_ref, tl_ref, back_ref):
    ph, pl_ = split(pair_ref[...])
    mixed = dot(th_ref[...], ph) + (dot(th_ref[...], pl_) + dot(tl_ref[...], ph))
    wh, wl = split(mixed * screened_ref[...])
    back_ref[...] = dot(vh_ref[...], wh) + (dot(vh_ref[...], wl) + dot(vl_ref[...], wh))


def direct_kernel(where_ref, terms_ref, ch_ref, cl_ref, out_ref):
    bh, bl = split(jnp.sum(terms_ref[...], axis=0))
    ch, cl = ch_ref[...], cl_ref[...]
    direct = dot_nt(bh, ch) + (dot_nt(bl, ch) + dot_nt(bh, cl))
    half, width = out_ref.shape[1:]
    left = lax.broadcasted_iota(jnp.int32, (half, width), 1) < width // 2
    for place in range(NX * NZ):
        q = where_ref[place]
        upper = direct[:half, place * width : (place + 1) * width]
        lower = direct[half:, place * width : (place + 1) * width]
        out_ref[2 * q] = jnp.where(left, upper, pltpu.roll(lower, width // 2, 1))
        out_ref[2 * q + 1] = jnp.where(left, pltpu.roll(upper, width // 2, 1), lower)


def scaled(terms_ref, vec, ediff_ref):
    hamil = ediff_ref[...] * vec - jnp.sum(terms_ref[...], axis=0)
    return (hamil - CENTER * vec) / HALF_WIDTH


def first_kernel(terms_ref, vec_ref, ediff_ref, new_ref, copies_ref):
    new = scaled(terms_ref, vec_ref[...], ediff_ref)
    new_ref[...] = new
    copies_ref[...] = jnp.broadcast_to(new[None], copies_ref.shape)


def last_kernel(terms_ref, vec_ref, older_ref, ediff_ref, out_ref):
    new = 2.0 * scaled(terms_ref, vec_ref[...], ediff_ref) - older_ref[...]
    half, width = new.shape
    out_ref[:half, :] = new[:, : width // 2]
    out_ref[half:, :] = new[:, width // 2 :]


def call(kernel, out_shapes, operands, scratch=(), far=()):
    shapes = [jax.ShapeDtypeStruct(s, d) for s, d in out_shapes]
    spaces = [pltpu.SMEM if a.dtype == jnp.int32 else pltpu.VMEM for a in operands]
    for i in far:
        spaces[i] = pltpu.HBM
        operands[i] = pltpu.with_memory_space_constraint(operands[i], pltpu.HBM)
    return pl.pallas_call(
        kernel,
        out_shape=shapes if len(shapes) > 1 else shapes[0],
        scratch_shapes=list(scratch),
        in_specs=[pl.BlockSpec(memory_space=space) for space in spaces],
        compiler_params=PARAMS,
    )(*operands)


def per_device(vectors, eval_energy, cond_energy, val_orbitals, cond_orbitals, screened):
    _, rows, cols = vectors.shape
    pts, val = lax.axis_size(PTS), lax.axis_size(VAL)
    depth_c, points_c = cond_orbitals.shape
    depth_v, points_v = val_orbitals.shape
    nv, nc = rows * val, cols * pts
    half, width = rows // 2, cols * 2

    x, core = lax.axis_index("x"), lax.axis_index("core")
    steps = jnp.arange(NX * NZ)
    chips = steps % NZ * NX + ((x - steps // NZ) & (NX - 1))
    ny = lax.axis_size("y")
    slots = steps % ny * 2 + (steps // ny ^ lax.axis_index("zh"))
    where = jnp.concatenate([chips, core[None], slots]).astype(jnp.int32)
    older = packed(vectors[0])
    ediff = packed(cond_energy[None, :] - eval_energy[:, None])

    mine = copied(cond_orbitals, "zl").reshape(-1, points_c)
    parcel = jnp.concatenate([val_orbitals, older], axis=1)
    parcel = jnp.concatenate([parcel, shifted(parcel, "zh", 1)], axis=0)
    mine, parcel = lax.optimization_barrier((mine, parcel))
    own = copied(parcel, "y").reshape(-1, depth_v, points_v + width)
    other = shifted(own, "core", 1)
    left, right = shifted(mine, "x", 1), shifted(mine, "x", -1)
    part = mine.shape[0] // 2
    upper, lower = shifted(left[:part], "x", 1), shifted(right[part:], "x", -1)

    newer = older
    scratch = [pltpu.VMEM((rows, nc), BF16)] * 2
    pair, ch, cl, vh, vl, th, tl, ediff, older = call(
        begin_kernel,
        [((val, rows, points_c), F32)]
        + [((nc, points_c), BF16)] * 2
        + [((nv, points_v), BF16)] * 2
        + [((points_v, nv), BF16)] * 2
        + [((half, width), F32)] * 2,
        [where, own, other, ediff, older, mine, left, upper, lower, right],
        [pltpu.VMEM(own.shape, F32)] * 2
        + [pltpu.VMEM((nc, points_c), F32)]
        + scratch
        + [pltpu.SemaphoreType.DMA((7,))],
        far=(1, 2, 5, 6, 7, 8, 9),
    )
    for step in range(ITERS):
        if step > 0:
            pair = call(
                pair_kernel,
                [((val, rows, points_c), F32)],
                [where, exchange(copies, PTS), ch, cl],
                scratch,
            )
        pair_all = exchange(pair, VAL).reshape(nv, points_c)
        back = call(
            screen_kernel, [((nv, points_c), F32)], [pair_all, screened, vh, vl, th, tl]
        )
        back = exchange(back.reshape(val, rows, points_c), VAL)
        direct = call(direct_kernel, [((pts, half, width), F32)], [where, back, ch, cl])
        direct = exchange(direct, PTS)
        if step < ITERS - 1:
            newer, copies = call(
                first_kernel,
                [((half, width), F32), ((pts, half, width), F32)],
                [direct, older, ediff],
            )
    out = call(last_kernel, [((rows, cols), F32)], [direct, newer, older, ediff])
    return out[None]


def solution(mesh):
    torus = Mesh(mesh.devices.reshape(2, 8, 2, 4, 4), ("zh", "y", "core", "zl", "x"))
    placed = (P(None, VAL, PTS), P(VAL), P(PTS), P(PTS, VAL), P(VAL, PTS), P(VAL, PTS))
    return jax.shard_map(
        per_device, mesh=torus, in_specs=placed, out_specs=P(None, VAL, PTS), check_vma=False
    )
```

```python
import jax
import jax.numpy as jnp
from jax import lax
from jax.experimental import pallas as pl
from jax.experimental.pallas import tpu as pltpu
from jax.sharding import Mesh
from jax.sharding import PartitionSpec as P

ITERS = 2
CENTER = 2.2
HALF_WIDTH = 2.0

ROWS = ("zh", "y")
PTS = ("zh", "y", "core")
Z, X = ("zl_hi", "zl_lo"), ("x_hi", "x_lo")
VAL = Z + X
CROSS = ("zh", "core")

NY, NZ, NX = 8, 4, 4
SEND = ("x_lo", "x_hi", "zl_lo", "zl_hi")
SENT = [int(f"{i:04b}"[::-1], 2) for i in range(NX * NZ)]

F32 = jnp.float32
BF16 = jnp.bfloat16
PARAMS = pltpu.CompilerParams(vmem_limit_bytes=20 * 1024 * 1024)


def split(a):
    hi = a.astype(BF16)
    return hi, (a - hi.astype(F32)).astype(BF16)


def dot(a, b):
    return jnp.dot(a, b, preferred_element_type=F32)


def dot_nt(a, b):
    return lax.dot_general(a, b, (((1,), (1,)), ((), ())), preferred_element_type=F32)


def exchange(blocks, axes):
    return lax.all_to_all(blocks, axes, 0, 0, tiled=True)


def shifted(array, axis, by):
    n = lax.axis_size(axis)
    if axis == CROSS:
        pairs = [(i, i ^ by) for i in range(n)]
    else:
        pairs = [(i, (i + by) % n) for i in range(n)]
    return lax.ppermute(array, axis, pairs)


def copied(array, axes):
    return exchange(jnp.broadcast_to(array[None], (lax.axis_size(axes), *array.shape)), axes)


def packed(block):
    half = block.shape[0] // 2
    return jnp.concatenate([block[:half], block[half:]], axis=1)


def place_pair(a, b, chip, xh_ref, xl_ref):
    half, width = a.shape
    left = lax.broadcasted_iota(jnp.int32, (half, width), 1) < width // 2
    upper = jnp.where(left, a, pltpu.roll(b, width // 2, 1))
    lower = jnp.where(left, pltpu.roll(a, width // 2, 1), b)
    cols = slice(chip * width, (chip + 1) * width)
    for part, rows in ((upper, slice(0, half)), (lower, slice(half, 2 * half))):
        hi, lo = split(part)
        xh_ref[rows, cols] = hi
        xl_ref[rows, cols] = lo


def collect(sources, target_ref, sems, first=0):
    copies = [
        pltpu.make_async_copy(source, target_ref.at[i], sems.at[first + i])
        for i, source in enumerate(sources)
    ]
    for copy in copies:
        copy.start()
    return copies


def begin_kernel(where_ref, ediff_ref, older_ref, own_hbm, other_hbm, *refs):
    conds, refs = refs[: NX + 1], refs[NX + 1 :]
    (pair_ref, ch_ref, cl_ref, vh_ref, vl_ref, th_ref, tl_ref, ediff_out_ref, older_out_ref,
     blocks_ref, cond_ref, xh_ref, xl_ref, block_sems, cond_sems) = refs
    parts = collect((own_hbm, other_hbm), blocks_ref, block_sems)
    part = conds[2].shape[0]
    places = [cond_ref.at[0], cond_ref.at[1], cond_ref.at[2, :part], cond_ref.at[2, part:]]
    conds = [
        pltpu.make_async_copy(ref, place, cond_sems.at[i])
        for i, (ref, place) in enumerate(zip(conds, places + [cond_ref.at[3]]))
    ]
    for copy in conds:
        copy.start()
    ediff_out_ref[...] = ediff_ref[...]
    older_out_ref[...] = older_ref[...]
    for copy in parts:
        copy.wait()
    points = vh_ref.shape[1]

    def block(p):
        return blocks_ref[where_ref[1 + p], where_ref[1 + 2 * NX * NZ + p // 2]]

    for q in range(NX * NZ):
        place_pair(block(2 * q)[:, points:], block(2 * q + 1)[:, points:], q, xh_ref, xl_ref)
    rows = [block(2 * q + half)[:, :points] for q in SENT for half in range(2)]
    whole = jnp.concatenate(rows, axis=0)
    hi, lo = split(whole)
    vh_ref[...] = hi
    vl_ref[...] = lo
    hi, lo = split(whole.T)
    th_ref[...] = hi
    tl_ref[...] = lo
    depth = cond_ref.shape[1] // NZ
    for copy in conds:
        copy.wait()
    for step in range(NX):
        for z in range(NZ):
            chip = z * NX + ((where_ref[0] - step) & (NX - 1))
            rows = pl.ds(pl.multiple_of(chip * depth, depth), depth)
            hi, lo = split(cond_ref[step, z * depth : (z + 1) * depth])
            ch_ref[rows, :] = hi
            cl_ref[rows, :] = lo
    multiply_pair(xh_ref, xl_ref, ch_ref, cl_ref, pair_ref)


def multiply_pair(xh_ref, xl_ref, ch_ref, cl_ref, pair_ref):
    ch, cl = ch_ref[...], cl_ref[...]
    pair = dot(xh_ref[...], ch) + (dot(xh_ref[...], cl) + dot(xl_ref[...], ch))
    pair_ref[...] = jnp.broadcast_to(pair[None], pair_ref.shape)


def pair_kernel(gathered_ref, ch_ref, cl_ref, pair_ref, xh_ref, xl_ref):
    for q in range(NX * NZ):
        place_pair(gathered_ref[2 * q], gathered_ref[2 * q + 1], q, xh_ref, xl_ref)
    multiply_pair(xh_ref, xl_ref, ch_ref, cl_ref, pair_ref)


def screen_kernel(pair_ref, screened_ref, vh_ref, vl_ref, th_ref, tl_ref, back_ref):
    ph, pl_ = split(pair_ref[...])
    mixed = dot(th_ref[...], ph) + (dot(th_ref[...], pl_) + dot(tl_ref[...], ph))
    wh, wl = split(mixed * screened_ref[...])
    back_ref[...] = dot(vh_ref[...], wh) + (dot(vh_ref[...], wl) + dot(vl_ref[...], wh))


def direct_kernel(terms_ref, ch_ref, cl_ref, out_ref):
    bh, bl = split(jnp.sum(terms_ref[...], axis=0))
    ch, cl = ch_ref[...], cl_ref[...]
    direct = dot_nt(bh, ch) + (dot_nt(bl, ch) + dot_nt(bh, cl))
    half, width = out_ref.shape[1:]
    left = lax.broadcasted_iota(jnp.int32, (half, width), 1) < width // 2
    for q in range(NX * NZ):
        upper = direct[:half, q * width : (q + 1) * width]
        lower = direct[half:, q * width : (q + 1) * width]
        out_ref[2 * q] = jnp.where(left, upper, pltpu.roll(lower, width // 2, 1))
        out_ref[2 * q + 1] = jnp.where(left, pltpu.roll(upper, width // 2, 1), lower)


def scaled(terms_ref, vec, ediff_ref):
    hamil = ediff_ref[...] * vec - jnp.sum(terms_ref[...], axis=0)
    return (hamil - CENTER * vec) / HALF_WIDTH


def first_kernel(terms_ref, vec_ref, ediff_ref, new_ref, copies_ref):
    new = scaled(terms_ref, vec_ref[...], ediff_ref)
    new_ref[...] = new
    copies_ref[...] = jnp.broadcast_to(new[None], copies_ref.shape)


def last_kernel(terms_ref, vec_ref, older_ref, ediff_ref, out_ref):
    new = 2.0 * scaled(terms_ref, vec_ref[...], ediff_ref) - older_ref[...]
    half, width = new.shape
    out_ref[:half, :] = new[:, : width // 2]
    out_ref[half:, :] = new[:, width // 2 :]


def call(kernel, out_shapes, operands, scratch=(), far=()):
    shapes = [jax.ShapeDtypeStruct(s, d) for s, d in out_shapes]
    spaces = [pltpu.SMEM if a.dtype == jnp.int32 else pltpu.VMEM for a in operands]
    for i in far:
        spaces[i] = pltpu.HBM
        operands[i] = pltpu.with_memory_space_constraint(operands[i], pltpu.HBM)
    return pl.pallas_call(
        kernel,
        out_shape=shapes if len(shapes) > 1 else shapes[0],
        scratch_shapes=list(scratch),
        in_specs=[pl.BlockSpec(memory_space=space) for space in spaces],
        compiler_params=PARAMS,
    )(*operands)


def per_device(vectors, eval_energy, cond_energy, val_orbitals, cond_orbitals, screened):
    _, rows, cols = vectors.shape
    pts, val = lax.axis_size(PTS), lax.axis_size(VAL)
    depth_c, points_c = cond_orbitals.shape
    depth_v, points_v = val_orbitals.shape
    nv, nc = rows * val, cols * pts
    half, width = rows // 2, cols * 2

    zh, core = lax.axis_index("zh"), lax.axis_index("core")
    p = jnp.arange(pts)
    chip = jnp.arange(val)
    where = [lax.axis_index(X)[None], (p & 1) ^ core, chip % NY * 2 + (chip // NY ^ zh)]
    where = jnp.concatenate(where).astype(jnp.int32)
    older = packed(vectors[0])
    ediff = packed(cond_energy[None, :] - eval_energy[:, None])

    mine = copied(cond_orbitals, Z).reshape(-1, points_c)
    parcel = jnp.concatenate([val_orbitals, older], axis=1)
    parcel = jnp.concatenate([parcel, shifted(parcel, "zh", 1)], axis=0)
    mine, parcel = lax.optimization_barrier((mine, parcel))
    own = copied(parcel, "y").reshape(-1, depth_v, points_v + width)
    other = shifted(own, "core", 1)
    left, right = shifted(mine, X, 1), shifted(mine, X, -1)
    part = mine.shape[0] // 2
    upper, lower = shifted(left[:part], X, 1), shifted(right[part:], X, -1)
    cond = [mine, left, upper, lower, right]

    newer = older
    scratch = [pltpu.VMEM((rows, nc), BF16)] * 2
    pair, ch, cl, vh, vl, th, tl, ediff, older = call(
        begin_kernel,
        [((val, rows, points_c), F32)]
        + [((nc, points_c), BF16)] * 2
        + [((nv, points_v), BF16)] * 2
        + [((points_v, nv), BF16)] * 2
        + [((half, width), F32)] * 2,
        [where, ediff, older, own, other, *cond],
        [pltpu.VMEM((2, *own.shape), F32), pltpu.VMEM((NX, *mine.shape), F32)]
        + scratch
        + [pltpu.SemaphoreType.DMA((2,)), pltpu.SemaphoreType.DMA((NX + 1,))],
        far=range(3, 6 + NX),
    )
    for step in range(ITERS):
        if step > 0:
            pair = call(
                pair_kernel,
                [((val, rows, points_c), F32)],
                [exchange(copies, PTS), ch, cl],
                scratch,
            )
        pair_all = exchange(pair, SEND).reshape(nv, points_c)
        back = call(
            screen_kernel, [((nv, points_c), F32)], [pair_all, screened, vh, vl, th, tl]
        )
        back = exchange(back.reshape(val, rows, points_c), SEND)
        direct = call(direct_kernel, [((pts, half, width), F32)], [back, ch, cl])
        direct = exchange(direct, PTS)
        if step < ITERS - 1:
            newer, copies = call(
                first_kernel,
                [((half, width), F32), ((pts, half, width), F32)],
                [direct, older, ediff],
            )
    out = call(last_kernel, [((rows, cols), F32)], [direct, newer, older, ediff])
    return out[None]


def solution(mesh):
    torus = Mesh(mesh.devices.reshape(2, 8, 2, 2, 2, 2, 2), PTS + Z + X)
    placed = (P(None, VAL, PTS), P(VAL), P(PTS), P(PTS, VAL), P(VAL, PTS), P(VAL, PTS))
    return jax.shard_map(
        per_device, mesh=torus, in_specs=placed, out_specs=P(None, VAL, PTS), check_vma=False
    )
```

```python
import jax
import jax.numpy as jnp
from jax import lax
from jax.experimental import pallas as pl
from jax.experimental.pallas import tpu as pltpu
from jax.sharding import Mesh
from jax.sharding import PartitionSpec as P

ITERS = 2
CENTER = 2.2
HALF_WIDTH = 2.0

ROWS = ("zh", "y")
PTS = ("zh", "y", "core")
Z, X = ("zl_hi", "zl_lo"), ("x_hi", "x_lo")
VAL = Z + X
CROSS = ("zh", "core")

NY, NZ, NX = 8, 4, 4
EARLY, LATE = (0, 1, 3), (2,)
WIDTH = 128
SEND = ("x_lo", "x_hi", "zl_lo", "zl_hi")
SWEEP = ("y", "core", "zh")
SENT = [int(f"{i:04b}"[::-1], 2) for i in range(NX * NZ)]

F32 = jnp.float32
BF16 = jnp.bfloat16
PARAMS = pltpu.CompilerParams(vmem_limit_bytes=20 * 1024 * 1024)


def split(a):
    hi = a.astype(BF16)
    return hi, (a - hi.astype(F32)).astype(BF16)


def dot(a, b):
    return jnp.dot(a, b, preferred_element_type=F32)


def dot_nt(a, b):
    return lax.dot_general(a, b, (((1,), (1,)), ((), ())), preferred_element_type=F32)


def exchange(blocks, axes):
    return lax.all_to_all(blocks, axes, 0, 0, tiled=True)


def shifted(array, axis, by):
    n = lax.axis_size(axis)
    if axis == CROSS:
        pairs = [(i, i ^ by) for i in range(n)]
    else:
        pairs = [(i, (i + by) % n) for i in range(n)]
    return lax.ppermute(array, axis, pairs)


def copied(array, axes):
    return exchange(jnp.broadcast_to(array[None], (lax.axis_size(axes), *array.shape)), axes)


def packed(block):
    half = block.shape[0] // 2
    return jnp.concatenate([block[:half], block[half:]], axis=1)


def sent_at(p):
    return p % (2 * NY) * 2 + p // (2 * NY)


def place_pair(a, b, chip, xh_ref, xl_ref):
    half, width = a.shape
    left = lax.broadcasted_iota(jnp.int32, (half, width), 1) < width // 2
    upper = jnp.where(left, a, pltpu.roll(b, width // 2, 1))
    lower = jnp.where(left, pltpu.roll(a, width // 2, 1), b)
    cols = slice(chip * width, (chip + 1) * width)
    for part, rows in ((upper, slice(0, half)), (lower, slice(half, 2 * half))):
        hi, lo = split(part)
        xh_ref[rows, cols] = hi
        xl_ref[rows, cols] = lo


def collect(sources, target_ref, sems, first=0):
    copies = [
        pltpu.make_async_copy(source, target_ref.at[i], sems.at[first + i])
        for i, source in enumerate(sources)
    ]
    for copy in copies:
        copy.start()
    return copies


def block_of(where_ref, blocks_ref, p):
    return blocks_ref[where_ref[1 + p], where_ref[1 + 2 * NX * NZ + p // 2]]


def chip_at(where_ref, step, z):
    return z * NX + ((where_ref[0] - step) & (NX - 1))


def split_rows(where_ref, step, block, ch_ref, cl_ref):
    hi, lo = split(block)
    depth = block.shape[0] // NZ
    for z in range(NZ):
        at = pl.multiple_of(chip_at(where_ref, step, z) * depth, depth)
        ch_ref[pl.ds(at, depth), :] = hi[z * depth : (z + 1) * depth]
        cl_ref[pl.ds(at, depth), :] = lo[z * depth : (z + 1) * depth]
    return hi, lo


def early_kernel(where_ref, ediff_ref, older_ref, own_hbm, other_hbm, *refs):
    conds, refs = refs[: len(EARLY)], refs[len(EARLY) :]
    (vh_ref, vl_ref, th_ref, tl_ref, ch_ref, cl_ref, part_ref, far_h_ref, far_l_ref,
     ediff_out_ref, older_out_ref,
     blocks_ref, cond_ref, xh_ref, xl_ref, block_sems, cond_sems) = refs
    parts = collect((own_hbm, other_hbm), blocks_ref, block_sems)
    conds = collect(conds, cond_ref, cond_sems)
    ediff_out_ref[...] = ediff_ref[...]
    older_out_ref[...] = older_ref[...]
    for copy in parts:
        copy.wait()
    for i, step in enumerate(EARLY + LATE):
        for z in range(NZ):
            chip = chip_at(where_ref, step, z)
            a, b = (
                block_of(where_ref, blocks_ref, 2 * chip + core)[:, -WIDTH:] for core in range(2)
            )
            place_pair(a, b, i * NZ + z, xh_ref, xl_ref)
    points = vh_ref.shape[1]
    rows = [
        block_of(where_ref, blocks_ref, 2 * q + core)[:, :points] for q in SENT for core in range(2)
    ]
    whole = jnp.concatenate(rows, axis=0)
    hi, lo = split(whole)
    vh_ref[...] = hi
    vl_ref[...] = lo
    hi, lo = split(whole.T)
    th_ref[...] = hi
    tl_ref[...] = lo
    far_h_ref[...] = xh_ref[:, len(EARLY) * NZ * WIDTH :]
    far_l_ref[...] = xl_ref[:, len(EARLY) * NZ * WIDTH :]
    total = jnp.zeros_like(part_ref)
    for i, step in enumerate(EARLY):
        conds[i].wait()
        ch, cl = split_rows(where_ref, step, cond_ref[i], ch_ref, cl_ref)
        cols = slice(i * NZ * WIDTH, (i + 1) * NZ * WIDTH)
        xh, xl = xh_ref[:, cols], xl_ref[:, cols]
        total += dot(xh, ch) + (dot(xh, cl) + dot(xl, ch))
    part_ref[...] = total


def late_kernel(
    where_ref, part_ref, far_h_ref, far_l_ref, upper_hbm, lower_hbm, ch_in_ref, cl_in_ref,
    pair_ref, ch_ref, cl_ref, cond_ref, sems,
):
    del ch_in_ref, cl_in_ref
    for copy in collect((upper_hbm, lower_hbm), cond_ref, sems):
        copy.wait()
    block = cond_ref[...].reshape(-1, cond_ref.shape[2])
    ch, cl = split_rows(where_ref, LATE[0], block, ch_ref, cl_ref)
    xh, xl = far_h_ref[...], far_l_ref[...]
    pair = part_ref[...] + (dot(xh, ch) + (dot(xh, cl) + dot(xl, ch)))
    pair_ref[...] = jnp.broadcast_to(pair[None], pair_ref.shape)


def multiply_pair(xh_ref, xl_ref, ch_ref, cl_ref, pair_ref):
    ch, cl = ch_ref[...], cl_ref[...]
    pair = dot(xh_ref[...], ch) + (dot(xh_ref[...], cl) + dot(xl_ref[...], ch))
    pair_ref[...] = jnp.broadcast_to(pair[None], pair_ref.shape)


def pair_kernel(gathered_ref, ch_ref, cl_ref, pair_ref, xh_ref, xl_ref):
    for q in range(NX * NZ):
        a, b = gathered_ref[sent_at(2 * q)], gathered_ref[sent_at(2 * q + 1)]
        place_pair(a, b, q, xh_ref, xl_ref)
    multiply_pair(xh_ref, xl_ref, ch_ref, cl_ref, pair_ref)


def screen_kernel(pair_ref, screened_ref, vh_ref, vl_ref, th_ref, tl_ref, back_ref):
    ph, pl_ = split(pair_ref[...])
    mixed = dot(th_ref[...], ph) + (dot(th_ref[...], pl_) + dot(tl_ref[...], ph))
    wh, wl = split(mixed * screened_ref[...])
    back_ref[...] = dot(vh_ref[...], wh) + (dot(vh_ref[...], wl) + dot(vl_ref[...], wh))


def direct_kernel(terms_ref, ch_ref, cl_ref, out_ref):
    bh, bl = split(jnp.sum(terms_ref[...], axis=0))
    ch, cl = ch_ref[...], cl_ref[...]
    direct = dot_nt(bh, ch) + (dot_nt(bl, ch) + dot_nt(bh, cl))
    half, width = out_ref.shape[1:]
    left = lax.broadcasted_iota(jnp.int32, (half, width), 1) < width // 2
    for q in range(NX * NZ):
        upper = direct[:half, q * width : (q + 1) * width]
        lower = direct[half:, q * width : (q + 1) * width]
        out_ref[sent_at(2 * q)] = jnp.where(left, upper, pltpu.roll(lower, width // 2, 1))
        out_ref[sent_at(2 * q + 1)] = jnp.where(left, pltpu.roll(upper, width // 2, 1), lower)


def scaled(terms_ref, vec, ediff_ref):
    hamil = ediff_ref[...] * vec - jnp.sum(terms_ref[...], axis=0)
    return (hamil - CENTER * vec) / HALF_WIDTH


def first_kernel(terms_ref, vec_ref, ediff_ref, new_ref, copies_ref):
    new = scaled(terms_ref, vec_ref[...], ediff_ref)
    new_ref[...] = new
    copies_ref[...] = jnp.broadcast_to(new[None], copies_ref.shape)


def last_kernel(terms_ref, vec_ref, older_ref, ediff_ref, out_ref):
    new = 2.0 * scaled(terms_ref, vec_ref[...], ediff_ref) - older_ref[...]
    half, width = new.shape
    out_ref[:half, :] = new[:, : width // 2]
    out_ref[half:, :] = new[:, width // 2 :]


def call(kernel, out_shapes, operands, scratch=(), far=(), aliases=None):
    shapes = [jax.ShapeDtypeStruct(s, d) for s, d in out_shapes]
    spaces = [pltpu.SMEM if a.dtype == jnp.int32 else pltpu.VMEM for a in operands]
    for i in far:
        spaces[i] = pltpu.HBM
        operands[i] = pltpu.with_memory_space_constraint(operands[i], pltpu.HBM)
    return pl.pallas_call(
        kernel,
        out_shape=shapes if len(shapes) > 1 else shapes[0],
        scratch_shapes=list(scratch),
        in_specs=[pl.BlockSpec(memory_space=space) for space in spaces],
        input_output_aliases=aliases or {},
        compiler_params=PARAMS,
    )(*operands)


def per_device(vectors, eval_energy, cond_energy, val_orbitals, cond_orbitals, screened):
    _, rows, cols = vectors.shape
    pts, val = lax.axis_size(PTS), lax.axis_size(VAL)
    depth_c, points_c = cond_orbitals.shape
    depth_v, points_v = val_orbitals.shape
    nv, nc = rows * val, cols * pts
    half, width = rows // 2, cols * 2

    zh, core = lax.axis_index("zh"), lax.axis_index("core")
    p = jnp.arange(pts)
    chip = jnp.arange(val)
    where = [lax.axis_index(X)[None], (p & 1) ^ core, chip % NY * 2 + (chip // NY ^ zh)]
    where = jnp.concatenate(where).astype(jnp.int32)
    older = packed(vectors[0])
    ediff = packed(cond_energy[None, :] - eval_energy[:, None])

    mine = copied(cond_orbitals, Z).reshape(-1, points_c)
    parcel = jnp.concatenate([val_orbitals, older], axis=1)
    parcel = jnp.concatenate([parcel, shifted(parcel, "zh", 1)], axis=0)
    mine, parcel = lax.optimization_barrier((mine, parcel))
    own = copied(parcel, "y").reshape(-1, depth_v, points_v + width)
    other = shifted(own, "core", 1)
    left, right = shifted(mine, X, 1), shifted(mine, X, -1)
    part = mine.shape[0] // 2
    upper, lower = shifted(left[:part], X, 1), shifted(right[part:], X, -1)

    newer = older
    scratch = [pltpu.VMEM((rows, nc), BF16)] * 2
    far = nc // NX
    conds = [((nc, points_c), BF16)] * 2
    vh, vl, th, tl, ch, cl, pair, far_h, far_l, ediff, older = call(
        early_kernel,
        [((nv, points_v), BF16)] * 2
        + [((points_v, nv), BF16)] * 2
        + conds
        + [((rows, points_c), F32)]
        + [((rows, far), BF16)] * 2
        + [((half, width), F32)] * 2,
        [where, ediff, older, own, other, mine, left, right],
        [pltpu.VMEM((2, *own.shape), F32), pltpu.VMEM((len(EARLY), *mine.shape), F32)]
        + scratch
        + [pltpu.SemaphoreType.DMA((2,)), pltpu.SemaphoreType.DMA((len(EARLY),))],
        far=range(3, 8),
    )
    pair, ch, cl = call(
        late_kernel,
        [((val, rows, points_c), F32)] + conds,
        [where, pair, far_h, far_l, upper, lower, ch, cl],
        [pltpu.VMEM((2, *upper.shape), F32), pltpu.SemaphoreType.DMA((2,))],
        far=(4, 5),
        aliases={6: 1, 7: 2},
    )
    for step in range(ITERS):
        if step > 0:
            pair = call(
                pair_kernel,
                [((val, rows, points_c), F32)],
                [exchange(copies, SWEEP), ch, cl],
                scratch,
            )
        pair_all = exchange(pair, SEND).reshape(nv, points_c)
        back = call(
            screen_kernel, [((nv, points_c), F32)], [pair_all, screened, vh, vl, th, tl]
        )
        back = exchange(back.reshape(val, rows, points_c), SEND)
        direct = call(direct_kernel, [((pts, half, width), F32)], [back, ch, cl])
        direct = exchange(direct, SWEEP)
        if step < ITERS - 1:
            newer, copies = call(
                first_kernel,
                [((half, width), F32), ((pts, half, width), F32)],
                [direct, older, ediff],
            )
    out = call(last_kernel, [((rows, cols), F32)], [direct, newer, older, ediff])
    return out[None]


def solution(mesh):
    torus = Mesh(mesh.devices.reshape(2, 8, 2, 2, 2, 2, 2), PTS + Z + X)
    placed = (P(None, VAL, PTS), P(VAL), P(PTS), P(PTS, VAL), P(VAL, PTS), P(VAL, PTS))
    return jax.shard_map(
        per_device, mesh=torus, in_specs=placed, out_specs=P(None, VAL, PTS), check_vma=False
    )
```

```python
import jax
import jax.numpy as jnp
from jax import lax
from jax.experimental import pallas as pl
from jax.experimental.pallas import tpu as pltpu
from jax.sharding import Mesh
from jax.sharding import PartitionSpec as P

ITERS = 2
CENTER = 2.2
HALF_WIDTH = 2.0

ROWS = ("zh", "y")
PTS = ("zh", "y", "core")
Z, X = ("zl_hi", "zl_lo"), ("x_hi", "x_lo")
VAL = Z + X
CROSS = ("zh", "core")

NY, NZ, NX = 8, 4, 4
EARLY, LATE = (0, 1, 3), (2,)
WIDTH = 128
SEND = ("x_lo", "x_hi", "zl_lo", "zl_hi")
SWEEP = ("y", "core", "zh")
SENT = [int(f"{i:04b}"[::-1], 2) for i in range(NX * NZ)]

F32 = jnp.float32
BF16 = jnp.bfloat16
PARAMS = pltpu.CompilerParams(vmem_limit_bytes=20 * 1024 * 1024)


def split(a):
    hi = a.astype(BF16)
    return hi, (a - hi.astype(F32)).astype(BF16)


def dot(a, b):
    return jnp.dot(a, b, preferred_element_type=F32)


def dot_nt(a, b):
    return lax.dot_general(a, b, (((1,), (1,)), ((), ())), preferred_element_type=F32)


def exchange(blocks, axes):
    return lax.all_to_all(blocks, axes, 0, 0, tiled=True)


def shifted(array, axis, by):
    n = lax.axis_size(axis)
    if axis == CROSS:
        pairs = [(i, i ^ by) for i in range(n)]
    else:
        pairs = [(i, (i + by) % n) for i in range(n)]
    return lax.ppermute(array, axis, pairs)


def copied(array, axes):
    return exchange(jnp.broadcast_to(array[None], (lax.axis_size(axes), *array.shape)), axes)


def packed(block):
    half = block.shape[0] // 2
    return jnp.concatenate([block[:half], block[half:]], axis=1)


def sent_at(p):
    return p % (2 * NY) * 2 + p // (2 * NY)


def place_pair(a, b, chip, xh_ref, xl_ref):
    half, width = a.shape
    left = lax.broadcasted_iota(jnp.int32, (half, width), 1) < width // 2
    upper = jnp.where(left, a, pltpu.roll(b, width // 2, 1))
    lower = jnp.where(left, pltpu.roll(a, width // 2, 1), b)
    cols = slice(chip * width, (chip + 1) * width)
    for part, rows in ((upper, slice(0, half)), (lower, slice(half, 2 * half))):
        hi, lo = split(part)
        xh_ref[rows, cols] = hi
        xl_ref[rows, cols] = lo


def collect(sources, target_ref, sems, first=0):
    copies = [
        pltpu.make_async_copy(source, target_ref.at[i], sems.at[first + i])
        for i, source in enumerate(sources)
    ]
    for copy in copies:
        copy.start()
    return copies


def block_of(where_ref, blocks_ref, p):
    return blocks_ref[where_ref[1 + p], where_ref[1 + 2 * NX * NZ + p // 2]]


def chip_at(where_ref, step, z):
    return z * NX + ((where_ref[0] - step) & (NX - 1))


def split_rows(where_ref, step, block, ch_ref, cl_ref):
    hi, lo = split(block)
    depth = block.shape[0] // NZ
    for z in range(NZ):
        at = pl.multiple_of(chip_at(where_ref, step, z) * depth, depth)
        ch_ref[pl.ds(at, depth), :] = hi[z * depth : (z + 1) * depth]
        cl_ref[pl.ds(at, depth), :] = lo[z * depth : (z + 1) * depth]
    return hi, lo


def early_kernel(where_ref, ediff_ref, older_ref, own_hbm, other_hbm, *refs):
    conds, refs = refs[: len(EARLY)], refs[len(EARLY) :]
    (vh_ref, vl_ref, th_ref, tl_ref, ch_ref, cl_ref, part_ref, far_h_ref, far_l_ref,
     ediff_out_ref, older_out_ref,
     blocks_ref, cond_ref, xh_ref, xl_ref, block_sems, cond_sems) = refs
    parts = collect((own_hbm, other_hbm), blocks_ref, block_sems)
    conds = collect(conds, cond_ref, cond_sems)
    ediff_out_ref[...] = ediff_ref[...]
    older_out_ref[...] = older_ref[...]
    for copy in parts:
        copy.wait()
    for i, step in enumerate(EARLY + LATE):
        for z in range(NZ):
            chip = chip_at(where_ref, step, z)
            a, b = (
                block_of(where_ref, blocks_ref, 2 * chip + core)[:, -WIDTH:] for core in range(2)
            )
            place_pair(a, b, i * NZ + z, xh_ref, xl_ref)
    points = vh_ref.shape[1]
    rows = [
        block_of(where_ref, blocks_ref, 2 * q + core)[:, :points] for q in SENT for core in range(2)
    ]
    whole = jnp.concatenate(rows, axis=0)
    hi, lo = split(whole)
    vh_ref[...] = hi
    vl_ref[...] = lo
    hi, lo = split(whole.T)
    th_ref[...] = hi
    tl_ref[...] = lo
    far_h_ref[...] = xh_ref[:, len(EARLY) * NZ * WIDTH :]
    far_l_ref[...] = xl_ref[:, len(EARLY) * NZ * WIDTH :]
    total = jnp.zeros_like(part_ref)
    for i, step in enumerate(EARLY):
        conds[i].wait()
        ch, cl = split_rows(where_ref, step, cond_ref[i], ch_ref, cl_ref)
        cols = slice(i * NZ * WIDTH, (i + 1) * NZ * WIDTH)
        xh, xl = xh_ref[:, cols], xl_ref[:, cols]
        total += dot(xh, ch) + (dot(xh, cl) + dot(xl, ch))
    part_ref[...] = total


def late_kernel(
    where_ref, part_ref, far_h_ref, far_l_ref, upper_ref, lower_ref, ch_in_ref, cl_in_ref,
    pair_ref, ch_ref, cl_ref,
):
    del ch_in_ref, cl_in_ref
    block = jnp.concatenate([upper_ref[...], lower_ref[...]], axis=0)
    ch, cl = split_rows(where_ref, LATE[0], block, ch_ref, cl_ref)
    xh, xl = far_h_ref[...], far_l_ref[...]
    pair = part_ref[...] + (dot(xh, ch) + (dot(xh, cl) + dot(xl, ch)))
    pair_ref[...] = jnp.broadcast_to(pair[None], pair_ref.shape)


def multiply_pair(xh_ref, xl_ref, ch_ref, cl_ref, pair_ref):
    ch, cl = ch_ref[...], cl_ref[...]
    pair = dot(xh_ref[...], ch) + (dot(xh_ref[...], cl) + dot(xl_ref[...], ch))
    pair_ref[...] = jnp.broadcast_to(pair[None], pair_ref.shape)


def pair_kernel(gathered_ref, ch_ref, cl_ref, pair_ref, xh_ref, xl_ref):
    for q in range(NX * NZ):
        a, b = gathered_ref[sent_at(2 * q)], gathered_ref[sent_at(2 * q + 1)]
        place_pair(a, b, q, xh_ref, xl_ref)
    multiply_pair(xh_ref, xl_ref, ch_ref, cl_ref, pair_ref)


def screen_kernel(pair_ref, screened_ref, vh_ref, vl_ref, th_ref, tl_ref, back_ref):
    ph, pl_ = split(pair_ref[...])
    mixed = dot(th_ref[...], ph) + (dot(th_ref[...], pl_) + dot(tl_ref[...], ph))
    wh, wl = split(mixed * screened_ref[...])
    back_ref[...] = dot(vh_ref[...], wh) + (dot(vh_ref[...], wl) + dot(vl_ref[...], wh))


def direct_kernel(terms_ref, ch_ref, cl_ref, out_ref):
    bh, bl = split(jnp.sum(terms_ref[...], axis=0))
    ch, cl = ch_ref[...], cl_ref[...]
    direct = dot_nt(bh, ch) + (dot_nt(bl, ch) + dot_nt(bh, cl))
    half, width = out_ref.shape[1:]
    left = lax.broadcasted_iota(jnp.int32, (half, width), 1) < width // 2
    for q in range(NX * NZ):
        upper = direct[:half, q * width : (q + 1) * width]
        lower = direct[half:, q * width : (q + 1) * width]
        out_ref[sent_at(2 * q)] = jnp.where(left, upper, pltpu.roll(lower, width // 2, 1))
        out_ref[sent_at(2 * q + 1)] = jnp.where(left, pltpu.roll(upper, width // 2, 1), lower)


def scaled(terms_ref, vec, ediff_ref):
    hamil = ediff_ref[...] * vec - jnp.sum(terms_ref[...], axis=0)
    return (hamil - CENTER * vec) / HALF_WIDTH


def first_kernel(terms_ref, vec_ref, ediff_ref, new_ref, copies_ref):
    new = scaled(terms_ref, vec_ref[...], ediff_ref)
    new_ref[...] = new
    copies_ref[...] = jnp.broadcast_to(new[None], copies_ref.shape)


def last_kernel(terms_ref, vec_ref, older_ref, ediff_ref, out_ref):
    new = 2.0 * scaled(terms_ref, vec_ref[...], ediff_ref) - older_ref[...]
    half, width = new.shape
    out_ref[:half, :] = new[:, : width // 2]
    out_ref[half:, :] = new[:, width // 2 :]


def call(kernel, out_shapes, operands, scratch=(), far=(), aliases=None):
    shapes = [jax.ShapeDtypeStruct(s, d) for s, d in out_shapes]
    spaces = [pltpu.SMEM if a.dtype == jnp.int32 else pltpu.VMEM for a in operands]
    for i in far:
        spaces[i] = pltpu.HBM
        operands[i] = pltpu.with_memory_space_constraint(operands[i], pltpu.HBM)
    return pl.pallas_call(
        kernel,
        out_shape=shapes if len(shapes) > 1 else shapes[0],
        scratch_shapes=list(scratch),
        in_specs=[pl.BlockSpec(memory_space=space) for space in spaces],
        input_output_aliases=aliases or {},
        compiler_params=PARAMS,
    )(*operands)


def per_device(vectors, eval_energy, cond_energy, val_orbitals, cond_orbitals, screened):
    _, rows, cols = vectors.shape
    pts, val = lax.axis_size(PTS), lax.axis_size(VAL)
    depth_c, points_c = cond_orbitals.shape
    depth_v, points_v = val_orbitals.shape
    nv, nc = rows * val, cols * pts
    half, width = rows // 2, cols * 2

    zh, core = lax.axis_index("zh"), lax.axis_index("core")
    p = jnp.arange(pts)
    chip = jnp.arange(val)
    where = [lax.axis_index(X)[None], (p & 1) ^ core, chip % NY * 2 + (chip // NY ^ zh)]
    where = jnp.concatenate(where).astype(jnp.int32)
    older = packed(vectors[0])
    ediff = packed(cond_energy[None, :] - eval_energy[:, None])

    mine = copied(cond_orbitals, Z).reshape(-1, points_c)
    parcel = jnp.concatenate([val_orbitals, older], axis=1)
    parcel = jnp.concatenate([parcel, shifted(parcel, "zh", 1)], axis=0)
    mine, parcel = lax.optimization_barrier((mine, parcel))
    own = copied(parcel, "y").reshape(-1, depth_v, points_v + width)
    other = shifted(own, "core", 1)
    left, right = shifted(mine, X, 1), shifted(mine, X, -1)
    part = mine.shape[0] // 2
    upper, lower = shifted(left[:part], X, 1), shifted(right[part:], X, -1)

    newer = older
    scratch = [pltpu.VMEM((rows, nc), BF16)] * 2
    far = nc // NX
    conds = [((nc, points_c), BF16)] * 2
    vh, vl, th, tl, ch, cl, pair, far_h, far_l, ediff, older = call(
        early_kernel,
        [((nv, points_v), BF16)] * 2
        + [((points_v, nv), BF16)] * 2
        + conds
        + [((rows, points_c), F32)]
        + [((rows, far), BF16)] * 2
        + [((half, width), F32)] * 2,
        [where, ediff, older, own, other, mine, left, right],
        [pltpu.VMEM((2, *own.shape), F32), pltpu.VMEM((len(EARLY), *mine.shape), F32)]
        + scratch
        + [pltpu.SemaphoreType.DMA((2,)), pltpu.SemaphoreType.DMA((len(EARLY),))],
        far=range(3, 8),
    )
    pair, ch, cl = call(
        late_kernel,
        [((val, rows, points_c), F32)] + conds,
        [where, pair, far_h, far_l, upper, lower, ch, cl],
        aliases={6: 1, 7: 2},
    )
    for step in range(ITERS):
        if step > 0:
            pair = call(
                pair_kernel,
                [((val, rows, points_c), F32)],
                [exchange(copies, SWEEP), ch, cl],
                scratch,
            )
        pair_all = exchange(pair, SEND).reshape(nv, points_c)
        back = call(
            screen_kernel, [((nv, points_c), F32)], [pair_all, screened, vh, vl, th, tl]
        )
        back = exchange(back.reshape(val, rows, points_c), SEND)
        direct = call(direct_kernel, [((pts, half, width), F32)], [back, ch, cl])
        direct = exchange(direct, SWEEP)
        if step < ITERS - 1:
            newer, copies = call(
                first_kernel,
                [((half, width), F32), ((pts, half, width), F32)],
                [direct, older, ediff],
            )
    out = call(last_kernel, [((rows, cols), F32)], [direct, newer, older, ediff])
    return out[None]


def solution(mesh):
    torus = Mesh(mesh.devices.reshape(2, 8, 2, 2, 2, 2, 2), PTS + Z + X)
    placed = (P(None, VAL, PTS), P(VAL), P(PTS), P(PTS, VAL), P(VAL, PTS), P(VAL, PTS))
    return jax.shard_map(
        per_device, mesh=torus, in_specs=placed, out_specs=P(None, VAL, PTS), check_vma=False
    )
```

```python
import jax
import jax.numpy as jnp
from jax import lax
from jax.experimental import pallas as pl
from jax.experimental.pallas import tpu as pltpu
from jax.sharding import Mesh
from jax.sharding import PartitionSpec as P

ITERS = 2
CENTER = 2.2
HALF_WIDTH = 2.0

ROWS = ("zh", "y")
PTS = ("zh", "y", "core")
Z, X = ("zl_hi", "zl_lo"), ("x_hi", "x_lo")
VAL = Z + X
CROSS = ("zh", "core")

NY, NZ, NX = 8, 4, 4
EARLY, LATE = (0, 1, 3), (2,)
WIDTH = 128
SEND = ("x_lo", "x_hi", "zl_lo", "zl_hi")
SWEEP = ("y", "core", "zh")
SENT = [int(f"{i:04b}"[::-1], 2) for i in range(NX * NZ)]

F32 = jnp.float32
BF16 = jnp.bfloat16
PARAMS = pltpu.CompilerParams(vmem_limit_bytes=20 * 1024 * 1024)


def split(a):
    hi = a.astype(BF16)
    return hi, (a - hi.astype(F32)).astype(BF16)


def dot(a, b):
    return jnp.dot(a, b, preferred_element_type=F32)


def dot_nt(a, b):
    return lax.dot_general(a, b, (((1,), (1,)), ((), ())), preferred_element_type=F32)


def exchange(blocks, axes):
    return lax.all_to_all(blocks, axes, 0, 0, tiled=True)


def shifted(array, axis, by):
    n = lax.axis_size(axis)
    if axis == CROSS:
        pairs = [(i, i ^ by) for i in range(n)]
    else:
        pairs = [(i, (i + by) % n) for i in range(n)]
    return lax.ppermute(array, axis, pairs)


def copied(array, axes):
    return exchange(jnp.broadcast_to(array[None], (lax.axis_size(axes), *array.shape)), axes)


def packed(block):
    half = block.shape[0] // 2
    return jnp.concatenate([block[:half], block[half:]], axis=1)


def sent_at(p):
    return p % (2 * NY) * 2 + p // (2 * NY)


def place_pair(a, b, chip, xh_ref, xl_ref):
    half, width = a.shape
    left = lax.broadcasted_iota(jnp.int32, (half, width), 1) < width // 2
    upper = jnp.where(left, a, pltpu.roll(b, width // 2, 1))
    lower = jnp.where(left, pltpu.roll(a, width // 2, 1), b)
    cols = slice(chip * width, (chip + 1) * width)
    for part, rows in ((upper, slice(0, half)), (lower, slice(half, 2 * half))):
        hi, lo = split(part)
        xh_ref[rows, cols] = hi
        xl_ref[rows, cols] = lo


def collect(sources, target_ref, sems, first=0):
    copies = [
        pltpu.make_async_copy(source, target_ref.at[i], sems.at[first + i])
        for i, source in enumerate(sources)
    ]
    for copy in copies:
        copy.start()
    return copies


def block_of(where_ref, blocks_ref, p):
    return blocks_ref[where_ref[1 + p], where_ref[1 + 2 * NX * NZ + p // 2]]


def chip_at(where_ref, step, z):
    return z * NX + ((where_ref[0] - step) & (NX - 1))


def split_rows(where_ref, step, block, ch_ref, cl_ref):
    hi, lo = split(block)
    depth = block.shape[0] // NZ
    for z in range(NZ):
        at = pl.multiple_of(chip_at(where_ref, step, z) * depth, depth)
        ch_ref[pl.ds(at, depth), :] = hi[z * depth : (z + 1) * depth]
        cl_ref[pl.ds(at, depth), :] = lo[z * depth : (z + 1) * depth]
    return hi, lo


def early_kernel(where_ref, ediff_ref, older_ref, own_hbm, other_hbm, *refs):
    conds, refs = refs[: len(EARLY)], refs[len(EARLY) :]
    (vh_ref, vl_ref, th_ref, tl_ref, ch_ref, cl_ref, part_ref, far_h_ref, far_l_ref,
     ediff_out_ref, older_out_ref,
     blocks_ref, cond_ref, xh_ref, xl_ref, block_sems, cond_sems) = refs
    parts = collect((own_hbm, other_hbm), blocks_ref, block_sems)
    conds = collect(conds, cond_ref, cond_sems)
    ediff_out_ref[...] = ediff_ref[...]
    older_out_ref[...] = older_ref[...]
    for copy in parts:
        copy.wait()
    for i, step in enumerate(EARLY + LATE):
        for z in range(NZ):
            chip = chip_at(where_ref, step, z)
            a, b = (
                block_of(where_ref, blocks_ref, 2 * chip + core)[:, -WIDTH:] for core in range(2)
            )
            place_pair(a, b, i * NZ + z, xh_ref, xl_ref)
    points = vh_ref.shape[1]
    rows = [
        block_of(where_ref, blocks_ref, 2 * q + core)[:, :points] for q in SENT for core in range(2)
    ]
    whole = jnp.concatenate(rows, axis=0)
    hi, lo = split(whole)
    vh_ref[...] = hi
    vl_ref[...] = lo
    hi, lo = split(whole.T)
    th_ref[...] = hi
    tl_ref[...] = lo
    far_h_ref[...] = xh_ref[:, len(EARLY) * NZ * WIDTH :]
    far_l_ref[...] = xl_ref[:, len(EARLY) * NZ * WIDTH :]
    total = jnp.zeros_like(part_ref)
    for i, step in enumerate(EARLY):
        conds[i].wait()
        ch, cl = split_rows(where_ref, step, cond_ref[i], ch_ref, cl_ref)
        cols = slice(i * NZ * WIDTH, (i + 1) * NZ * WIDTH)
        xh, xl = xh_ref[:, cols], xl_ref[:, cols]
        total += dot(xh, ch) + (dot(xh, cl) + dot(xl, ch))
    part_ref[...] = total


def late_kernel(
    where_ref, part_ref, far_h_ref, far_l_ref, upper_ref, lower_ref, ch_in_ref, cl_in_ref,
    pair_ref, ch_ref, cl_ref,
):
    del ch_in_ref, cl_in_ref
    block = jnp.concatenate([upper_ref[...], lower_ref[...]], axis=0)
    ch, cl = split_rows(where_ref, LATE[0], block, ch_ref, cl_ref)
    xh, xl = far_h_ref[...], far_l_ref[...]
    pair = part_ref[...] + (dot(xh, ch) + (dot(xh, cl) + dot(xl, ch)))
    pair_ref[...] = jnp.broadcast_to(pair[None], pair_ref.shape)


def multiply_pair(xh_ref, xl_ref, ch_ref, cl_ref, pair_ref):
    ch, cl = ch_ref[...], cl_ref[...]
    pair = dot(xh_ref[...], ch) + (dot(xh_ref[...], cl) + dot(xl_ref[...], ch))
    pair_ref[...] = jnp.broadcast_to(pair[None], pair_ref.shape)


def pair_kernel(gathered_ref, ch_ref, cl_ref, pair_ref, xh_ref, xl_ref):
    for q in range(NX * NZ):
        a, b = gathered_ref[sent_at(2 * q)], gathered_ref[sent_at(2 * q + 1)]
        place_pair(a, b, q, xh_ref, xl_ref)
    multiply_pair(xh_ref, xl_ref, ch_ref, cl_ref, pair_ref)


def screen_kernel(pair_ref, screened_ref, vh_ref, vl_ref, th_ref, tl_ref, back_ref):
    ph, pl_ = split(pair_ref[...])
    half = th_ref.shape[0] // 2
    parts = []
    for at in (slice(0, half), slice(half, 2 * half)):
        th, tl = th_ref[at, :], tl_ref[at, :]
        mixed = dot(th, ph) + (dot(th, pl_) + dot(tl, ph))
        parts.append(split(mixed * screened_ref[at, :]))
    wh, wl = (jnp.concatenate(p, axis=0) for p in zip(*parts))
    back_ref[...] = dot(vh_ref[...], wh) + (dot(vh_ref[...], wl) + dot(vl_ref[...], wh))


def direct_kernel(terms_ref, ch_ref, cl_ref, out_ref):
    bh, bl = split(jnp.sum(terms_ref[...], axis=0))
    ch, cl = ch_ref[...], cl_ref[...]
    direct = dot_nt(bh, ch) + (dot_nt(bl, ch) + dot_nt(bh, cl))
    half, width = out_ref.shape[1:]
    left = lax.broadcasted_iota(jnp.int32, (half, width), 1) < width // 2
    for q in range(NX * NZ):
        upper = direct[:half, q * width : (q + 1) * width]
        lower = direct[half:, q * width : (q + 1) * width]
        out_ref[sent_at(2 * q)] = jnp.where(left, upper, pltpu.roll(lower, width // 2, 1))
        out_ref[sent_at(2 * q + 1)] = jnp.where(left, pltpu.roll(upper, width // 2, 1), lower)


def scaled(terms_ref, vec, ediff_ref):
    hamil = ediff_ref[...] * vec - jnp.sum(terms_ref[...], axis=0)
    return (hamil - CENTER * vec) / HALF_WIDTH


def first_kernel(terms_ref, vec_ref, ediff_ref, new_ref, copies_ref):
    new = scaled(terms_ref, vec_ref[...], ediff_ref)
    new_ref[...] = new
    copies_ref[...] = jnp.broadcast_to(new[None], copies_ref.shape)


def last_kernel(terms_ref, vec_ref, older_ref, ediff_ref, out_ref):
    new = 2.0 * scaled(terms_ref, vec_ref[...], ediff_ref) - older_ref[...]
    half, width = new.shape
    out_ref[:half, :] = new[:, : width // 2]
    out_ref[half:, :] = new[:, width // 2 :]


def call(kernel, out_shapes, operands, scratch=(), far=(), aliases=None):
    shapes = [jax.ShapeDtypeStruct(s, d) for s, d in out_shapes]
    spaces = [pltpu.SMEM if a.dtype == jnp.int32 else pltpu.VMEM for a in operands]
    for i in far:
        spaces[i] = pltpu.HBM
        operands[i] = pltpu.with_memory_space_constraint(operands[i], pltpu.HBM)
    return pl.pallas_call(
        kernel,
        out_shape=shapes if len(shapes) > 1 else shapes[0],
        scratch_shapes=list(scratch),
        in_specs=[pl.BlockSpec(memory_space=space) for space in spaces],
        input_output_aliases=aliases or {},
        compiler_params=PARAMS,
    )(*operands)


def per_device(vectors, eval_energy, cond_energy, val_orbitals, cond_orbitals, screened):
    _, rows, cols = vectors.shape
    pts, val = lax.axis_size(PTS), lax.axis_size(VAL)
    depth_c, points_c = cond_orbitals.shape
    depth_v, points_v = val_orbitals.shape
    nv, nc = rows * val, cols * pts
    half, width = rows // 2, cols * 2

    zh, core = lax.axis_index("zh"), lax.axis_index("core")
    p = jnp.arange(pts)
    chip = jnp.arange(val)
    where = [lax.axis_index(X)[None], (p & 1) ^ core, chip % NY * 2 + (chip // NY ^ zh)]
    where = jnp.concatenate(where).astype(jnp.int32)
    older = packed(vectors[0])
    ediff = packed(cond_energy[None, :] - eval_energy[:, None])

    mine = copied(cond_orbitals, Z).reshape(-1, points_c)
    parcel = jnp.concatenate([val_orbitals, older], axis=1)
    parcel = jnp.concatenate([parcel, shifted(parcel, "zh", 1)], axis=0)
    mine, parcel = lax.optimization_barrier((mine, parcel))
    own = copied(parcel, "y").reshape(-1, depth_v, points_v + width)
    other = shifted(own, "core", 1)
    left, right = shifted(mine, X, 1), shifted(mine, X, -1)
    part = mine.shape[0] // 2
    upper, lower = shifted(left[:part], X, 1), shifted(right[part:], X, -1)

    newer = older
    scratch = [pltpu.VMEM((rows, nc), BF16)] * 2
    far = nc // NX
    conds = [((nc, points_c), BF16)] * 2
    vh, vl, th, tl, ch, cl, pair, far_h, far_l, ediff, older = call(
        early_kernel,
        [((nv, points_v), BF16)] * 2
        + [((points_v, nv), BF16)] * 2
        + conds
        + [((rows, points_c), F32)]
        + [((rows, far), BF16)] * 2
        + [((half, width), F32)] * 2,
        [where, ediff, older, own, other, mine, left, right],
        [pltpu.VMEM((2, *own.shape), F32), pltpu.VMEM((len(EARLY), *mine.shape), F32)]
        + scratch
        + [pltpu.SemaphoreType.DMA((2,)), pltpu.SemaphoreType.DMA((len(EARLY),))],
        far=range(3, 8),
    )
    pair, ch, cl = call(
        late_kernel,
        [((val, rows, points_c), F32)] + conds,
        [where, pair, far_h, far_l, upper, lower, ch, cl],
        aliases={6: 1, 7: 2},
    )
    for step in range(ITERS):
        if step > 0:
            pair = call(
                pair_kernel,
                [((val, rows, points_c), F32)],
                [exchange(copies, SWEEP), ch, cl],
                scratch,
            )
        pair_all = exchange(pair, SEND).reshape(nv, points_c)
        back = call(
            screen_kernel, [((nv, points_c), F32)], [pair_all, screened, vh, vl, th, tl]
        )
        back = exchange(back.reshape(val, rows, points_c), SEND)
        direct = call(direct_kernel, [((pts, half, width), F32)], [back, ch, cl])
        direct = exchange(direct, SWEEP)
        if step < ITERS - 1:
            newer, copies = call(
                first_kernel,
                [((half, width), F32), ((pts, half, width), F32)],
                [direct, older, ediff],
            )
    out = call(last_kernel, [((rows, cols), F32)], [direct, newer, older, ediff])
    return out[None]


def solution(mesh):
    torus = Mesh(mesh.devices.reshape(2, 8, 2, 2, 2, 2, 2), PTS + Z + X)
    placed = (P(None, VAL, PTS), P(VAL), P(PTS), P(PTS, VAL), P(VAL, PTS), P(VAL, PTS))
    return jax.shard_map(
        per_device, mesh=torus, in_specs=placed, out_specs=P(None, VAL, PTS), check_vma=False
    )
```

```python
import jax
import jax.numpy as jnp
from jax import lax
from jax.experimental import pallas as pl
from jax.experimental.pallas import tpu as pltpu
from jax.sharding import Mesh
from jax.sharding import PartitionSpec as P

ITERS = 2
CENTER = 2.2
HALF_WIDTH = 2.0

Y = ("y_hi", "y_mid", "y_lo")
PTS = ("zh",) + Y + ("core",)
Z, X = ("zl_hi", "zl_lo"), ("x_hi", "x_lo")
VAL = Z + X
CROSS = ("zh", "core")

NY, NZ, NX = 8, 4, 4
EARLY, LATE = (0, 1, 3), (2,)
WIDTH = 128
SEND = ("x_lo", "x_hi", "zl_lo", "zl_hi")
SWEEP = Y + ("core", "zh")
SENT = [int(f"{i:04b}"[::-1], 2) for i in range(NX * NZ)]

F32 = jnp.float32
BF16 = jnp.bfloat16
PARAMS = pltpu.CompilerParams(vmem_limit_bytes=20 * 1024 * 1024)


def split(a):
    hi = a.astype(BF16)
    return hi, (a - hi.astype(F32)).astype(BF16)


def dot(a, b):
    return jnp.dot(a, b, preferred_element_type=F32)


def dot_nt(a, b):
    return lax.dot_general(a, b, (((1,), (1,)), ((), ())), preferred_element_type=F32)


def exchange(blocks, axes):
    return lax.all_to_all(blocks, axes, 0, 0, tiled=True)


def shifted(array, axis, by):
    n = lax.axis_size(axis)
    if axis == CROSS:
        pairs = [(i, i ^ by) for i in range(n)]
    else:
        pairs = [(i, (i + by) % n) for i in range(n)]
    return lax.ppermute(array, axis, pairs)


def copied(array, axes):
    return exchange(jnp.broadcast_to(array[None], (lax.axis_size(axes), *array.shape)), axes)


def packed(block):
    half = block.shape[0] // 2
    return jnp.concatenate([block[:half], block[half:]], axis=1)


def sent_at(p):
    return p % (2 * NY) * 2 + p // (2 * NY)


def place_pair(a, b, chip, xh_ref, xl_ref):
    half, width = a.shape
    left = lax.broadcasted_iota(jnp.int32, (half, width), 1) < width // 2
    upper = jnp.where(left, a, pltpu.roll(b, width // 2, 1))
    lower = jnp.where(left, pltpu.roll(a, width // 2, 1), b)
    cols = slice(chip * width, (chip + 1) * width)
    for part, rows in ((upper, slice(0, half)), (lower, slice(half, 2 * half))):
        hi, lo = split(part)
        xh_ref[rows, cols] = hi
        xl_ref[rows, cols] = lo


def collect(sources, target_ref, sems, first=0):
    copies = [
        pltpu.make_async_copy(source, target_ref.at[i], sems.at[first + i])
        for i, source in enumerate(sources)
    ]
    for copy in copies:
        copy.start()
    return copies


def block_of(where_ref, blocks_ref, p):
    return blocks_ref[where_ref[1 + p], where_ref[1 + 2 * NX * NZ + p // 2]]


def chip_at(where_ref, step, z):
    return z * NX + ((where_ref[0] - step) & (NX - 1))


def split_rows(where_ref, step, block, ch_ref, cl_ref):
    hi, lo = split(block)
    depth = block.shape[0] // NZ
    for z in range(NZ):
        at = pl.multiple_of(chip_at(where_ref, step, z) * depth, depth)
        ch_ref[pl.ds(at, depth), :] = hi[z * depth : (z + 1) * depth]
        cl_ref[pl.ds(at, depth), :] = lo[z * depth : (z + 1) * depth]
    return hi, lo


def early_kernel(where_ref, ediff_ref, older_ref, own_hbm, other_hbm, *refs):
    conds, refs = refs[: len(EARLY)], refs[len(EARLY) :]
    (vh_ref, vl_ref, th_ref, tl_ref, ch_ref, cl_ref, part_ref, far_h_ref, far_l_ref,
     ediff_out_ref, older_out_ref,
     blocks_ref, cond_ref, xh_ref, xl_ref, block_sems, cond_sems) = refs
    parts = collect((own_hbm, other_hbm), blocks_ref, block_sems)
    conds = collect(conds, cond_ref, cond_sems)
    ediff_out_ref[...] = ediff_ref[...]
    older_out_ref[...] = older_ref[...]
    for copy in parts:
        copy.wait()
    for i, step in enumerate(EARLY + LATE):
        for z in range(NZ):
            chip = chip_at(where_ref, step, z)
            a, b = (
                block_of(where_ref, blocks_ref, 2 * chip + core)[:, -WIDTH:] for core in range(2)
            )
            place_pair(a, b, i * NZ + z, xh_ref, xl_ref)
    points = vh_ref.shape[1]
    rows = [
        block_of(where_ref, blocks_ref, 2 * q + core)[:, :points] for q in SENT for core in range(2)
    ]
    whole = jnp.concatenate(rows, axis=0)
    hi, lo = split(whole)
    vh_ref[...] = hi
    vl_ref[...] = lo
    hi, lo = split(whole.T)
    th_ref[...] = hi
    tl_ref[...] = lo
    far_h_ref[...] = xh_ref[:, len(EARLY) * NZ * WIDTH :]
    far_l_ref[...] = xl_ref[:, len(EARLY) * NZ * WIDTH :]
    total = jnp.zeros_like(part_ref)
    for i, step in enumerate(EARLY):
        conds[i].wait()
        ch, cl = split_rows(where_ref, step, cond_ref[i], ch_ref, cl_ref)
        cols = slice(i * NZ * WIDTH, (i + 1) * NZ * WIDTH)
        xh, xl = xh_ref[:, cols], xl_ref[:, cols]
        total += dot(xh, ch) + (dot(xh, cl) + dot(xl, ch))
    part_ref[...] = total


def late_kernel(
    where_ref, part_ref, far_h_ref, far_l_ref, upper_ref, lower_ref, ch_in_ref, cl_in_ref,
    pair_ref, ch_ref, cl_ref,
):
    del ch_in_ref, cl_in_ref
    block = jnp.concatenate([upper_ref[...], lower_ref[...]], axis=0)
    ch, cl = split_rows(where_ref, LATE[0], block, ch_ref, cl_ref)
    xh, xl = far_h_ref[...], far_l_ref[...]
    pair = part_ref[...] + (dot(xh, ch) + (dot(xh, cl) + dot(xl, ch)))
    pair_ref[...] = jnp.broadcast_to(pair[None], pair_ref.shape)


def multiply_pair(xh_ref, xl_ref, ch_ref, cl_ref, pair_ref):
    ch, cl = ch_ref[...], cl_ref[...]
    pair = dot(xh_ref[...], ch) + (dot(xh_ref[...], cl) + dot(xl_ref[...], ch))
    pair_ref[...] = jnp.broadcast_to(pair[None], pair_ref.shape)


def pair_kernel(gathered_ref, ch_ref, cl_ref, pair_ref, xh_ref, xl_ref):
    for q in range(NX * NZ):
        a, b = gathered_ref[sent_at(2 * q)], gathered_ref[sent_at(2 * q + 1)]
        place_pair(a, b, q, xh_ref, xl_ref)
    multiply_pair(xh_ref, xl_ref, ch_ref, cl_ref, pair_ref)


def screen_kernel(pair_ref, screened_ref, vh_ref, vl_ref, th_ref, tl_ref, back_ref):
    ph, pl_ = split(pair_ref[...])
    half = th_ref.shape[0] // 2
    parts = []
    for at in (slice(0, half), slice(half, 2 * half)):
        th, tl = th_ref[at, :], tl_ref[at, :]
        mixed = dot(th, ph) + (dot(th, pl_) + dot(tl, ph))
        parts.append(split(mixed * screened_ref[at, :]))
    wh, wl = (jnp.concatenate(p, axis=0) for p in zip(*parts))
    back_ref[...] = dot(vh_ref[...], wh) + (dot(vh_ref[...], wl) + dot(vl_ref[...], wh))


def direct_kernel(terms_ref, ch_ref, cl_ref, out_ref):
    bh, bl = split(jnp.sum(terms_ref[...], axis=0))
    ch, cl = ch_ref[...], cl_ref[...]
    direct = dot_nt(bh, ch) + (dot_nt(bl, ch) + dot_nt(bh, cl))
    half, width = out_ref.shape[1:]
    left = lax.broadcasted_iota(jnp.int32, (half, width), 1) < width // 2
    for q in range(NX * NZ):
        upper = direct[:half, q * width : (q + 1) * width]
        lower = direct[half:, q * width : (q + 1) * width]
        out_ref[sent_at(2 * q)] = jnp.where(left, upper, pltpu.roll(lower, width // 2, 1))
        out_ref[sent_at(2 * q + 1)] = jnp.where(left, pltpu.roll(upper, width // 2, 1), lower)


def scaled(terms_ref, vec, ediff_ref):
    hamil = ediff_ref[...] * vec - jnp.sum(terms_ref[...], axis=0)
    return (hamil - CENTER * vec) / HALF_WIDTH


def first_kernel(terms_ref, vec_ref, ediff_ref, new_ref, copies_ref):
    new = scaled(terms_ref, vec_ref[...], ediff_ref)
    new_ref[...] = new
    copies_ref[...] = jnp.broadcast_to(new[None], copies_ref.shape)


def last_kernel(terms_ref, vec_ref, older_ref, ediff_ref, out_ref):
    new = 2.0 * scaled(terms_ref, vec_ref[...], ediff_ref) - older_ref[...]
    half, width = new.shape
    out_ref[:half, :] = new[:, : width // 2]
    out_ref[half:, :] = new[:, width // 2 :]


def call(kernel, out_shapes, operands, scratch=(), far=(), aliases=None):
    shapes = [jax.ShapeDtypeStruct(s, d) for s, d in out_shapes]
    spaces = [pltpu.SMEM if a.dtype == jnp.int32 else pltpu.VMEM for a in operands]
    for i in far:
        spaces[i] = pltpu.HBM
        operands[i] = pltpu.with_memory_space_constraint(operands[i], pltpu.HBM)
    return pl.pallas_call(
        kernel,
        out_shape=shapes if len(shapes) > 1 else shapes[0],
        scratch_shapes=list(scratch),
        in_specs=[pl.BlockSpec(memory_space=space) for space in spaces],
        input_output_aliases=aliases or {},
        compiler_params=PARAMS,
    )(*operands)


def per_device(vectors, eval_energy, cond_energy, val_orbitals, cond_orbitals, screened):
    _, rows, cols = vectors.shape
    pts, val = lax.axis_size(PTS), lax.axis_size(VAL)
    depth_c, points_c = cond_orbitals.shape
    depth_v, points_v = val_orbitals.shape
    nv, nc = rows * val, cols * pts
    half, width = rows // 2, cols * 2

    zh, core = lax.axis_index("zh"), lax.axis_index("core")
    p = jnp.arange(pts)
    chip = jnp.arange(val)
    where = [lax.axis_index(X)[None], (p & 1) ^ core, (chip & 1) * 8 + (chip & 2) * 2 + (chip & 4) // 2 + (chip // NY ^ zh)]
    where = jnp.concatenate(where).astype(jnp.int32)
    older = packed(vectors[0])
    ediff = packed(cond_energy[None, :] - eval_energy[:, None])

    mine = copied(cond_orbitals, Z).reshape(-1, points_c)
    parcel = jnp.concatenate([val_orbitals, older], axis=1)
    parcel = jnp.concatenate([parcel, shifted(parcel, "zh", 1)], axis=0)
    mine, parcel = lax.optimization_barrier((mine, parcel))
    own = copied(parcel, Y[::-1]).reshape(-1, depth_v, points_v + width)
    other = shifted(own, "core", 1)
    left, right = shifted(mine, X, 1), shifted(mine, X, -1)
    part = mine.shape[0] // 2
    upper, lower = shifted(left[:part], X, 1), shifted(right[part:], X, -1)

    newer = older
    scratch = [pltpu.VMEM((rows, nc), BF16)] * 2
    far = nc // NX
    conds = [((nc, points_c), BF16)] * 2
    vh, vl, th, tl, ch, cl, pair, far_h, far_l, ediff, older = call(
        early_kernel,
        [((nv, points_v), BF16)] * 2
        + [((points_v, nv), BF16)] * 2
        + conds
        + [((rows, points_c), F32)]
        + [((rows, far), BF16)] * 2
        + [((half, width), F32)] * 2,
        [where, ediff, older, own, other, mine, left, right],
        [pltpu.VMEM((2, *own.shape), F32), pltpu.VMEM((len(EARLY), *mine.shape), F32)]
        + scratch
        + [pltpu.SemaphoreType.DMA((2,)), pltpu.SemaphoreType.DMA((len(EARLY),))],
        far=range(3, 8),
    )
    pair, ch, cl = call(
        late_kernel,
        [((val, rows, points_c), F32)] + conds,
        [where, pair, far_h, far_l, upper, lower, ch, cl],
        aliases={6: 1, 7: 2},
    )
    for step in range(ITERS):
        if step > 0:
            pair = call(
                pair_kernel,
                [((val, rows, points_c), F32)],
                [exchange(copies, SWEEP), ch, cl],
                scratch,
            )
        pair_all = exchange(pair, SEND).reshape(nv, points_c)
        back = call(
            screen_kernel, [((nv, points_c), F32)], [pair_all, screened, vh, vl, th, tl]
        )
        back = exchange(back.reshape(val, rows, points_c), SEND)
        direct = call(direct_kernel, [((pts, half, width), F32)], [back, ch, cl])
        direct = exchange(direct, SWEEP)
        if step < ITERS - 1:
            newer, copies = call(
                first_kernel,
                [((half, width), F32), ((pts, half, width), F32)],
                [direct, older, ediff],
            )
    out = call(last_kernel, [((rows, cols), F32)], [direct, newer, older, ediff])
    return out[None]


def solution(mesh):
    torus = Mesh(mesh.devices.reshape((2,) * 9), PTS + Z + X)
    placed = (P(None, VAL, PTS), P(VAL), P(PTS), P(PTS, VAL), P(VAL, PTS), P(VAL, PTS))
    return jax.shard_map(
        per_device, mesh=torus, in_specs=placed, out_specs=P(None, VAL, PTS), check_vma=False
    )
```

```python
import jax
import jax.numpy as jnp
from jax import lax
from jax.experimental import pallas as pl
from jax.experimental.pallas import tpu as pltpu
from jax.sharding import Mesh
from jax.sharding import PartitionSpec as P

ITERS = 2
CENTER = 2.2
HALF_WIDTH = 2.0

ROWS = ("zh", "y")
PTS = ("zh", "y", "core")
Z, X = ("zl_hi", "zl_lo"), ("x_hi", "x_lo")
VAL = Z + X
CROSS = ("zh", "core")

NY, NZ, NX = 8, 4, 4
EARLY, LATE = (0, 1, 3), (2,)
WIDTH = 128
SEND = ("x_lo", "x_hi", "zl_lo", "zl_hi")
SWEEP = ("y", "core", "zh")
SENT = [int(f"{i:04b}"[::-1], 2) for i in range(NX * NZ)]

F32 = jnp.float32
BF16 = jnp.bfloat16
PARAMS = pltpu.CompilerParams(vmem_limit_bytes=20 * 1024 * 1024)


def split(a):
    hi = a.astype(BF16)
    return hi, (a - hi.astype(F32)).astype(BF16)


def dot(a, b):
    return jnp.dot(a, b, preferred_element_type=F32)


def dot_nt(a, b):
    return lax.dot_general(a, b, (((1,), (1,)), ((), ())), preferred_element_type=F32)


def exchange(blocks, axes):
    return lax.all_to_all(blocks, axes, 0, 0, tiled=True)


def shifted(array, axis, by):
    n = lax.axis_size(axis)
    if axis == CROSS:
        pairs = [(i, i ^ by) for i in range(n)]
    else:
        pairs = [(i, (i + by) % n) for i in range(n)]
    return lax.ppermute(array, axis, pairs)


def copied(array, axes):
    return exchange(jnp.broadcast_to(array[None], (lax.axis_size(axes), *array.shape)), axes)


def packed(block):
    half = block.shape[0] // 2
    return jnp.concatenate([block[:half], block[half:]], axis=1)


def sent_at(p):
    return p % (2 * NY) * 2 + p // (2 * NY)


def place_pair(a, b, chip, xh_ref, xl_ref):
    half, width = a.shape
    left = lax.broadcasted_iota(jnp.int32, (half, width), 1) < width // 2
    upper = jnp.where(left, a, pltpu.roll(b, width // 2, 1))
    lower = jnp.where(left, pltpu.roll(a, width // 2, 1), b)
    cols = slice(chip * width, (chip + 1) * width)
    for part, rows in ((upper, slice(0, half)), (lower, slice(half, 2 * half))):
        hi, lo = split(part)
        xh_ref[rows, cols] = hi
        xl_ref[rows, cols] = lo


def collect(sources, target_ref, sems, first=0):
    copies = [
        pltpu.make_async_copy(source, target_ref.at[i], sems.at[first + i])
        for i, source in enumerate(sources)
    ]
    for copy in copies:
        copy.start()
    return copies


def block_of(where_ref, blocks_ref, p):
    return blocks_ref[where_ref[1 + p], where_ref[1 + 2 * NX * NZ + p // 2]]


def chip_at(where_ref, step, z):
    return z * NX + ((where_ref[0] - step) & (NX - 1))


def split_rows(where_ref, step, block, ch_ref, cl_ref):
    hi, lo = split(block)
    depth = block.shape[0] // NZ
    for z in range(NZ):
        at = pl.multiple_of(chip_at(where_ref, step, z) * depth, depth)
        ch_ref[pl.ds(at, depth), :] = hi[z * depth : (z + 1) * depth]
        cl_ref[pl.ds(at, depth), :] = lo[z * depth : (z + 1) * depth]
    return hi, lo


def early_kernel(where_ref, ediff_ref, older_ref, own_hbm, other_hbm, *refs):
    conds, refs = refs[: len(EARLY)], refs[len(EARLY) :]
    (vh_ref, vl_ref, th_ref, tl_ref, ch_ref, cl_ref, part_ref, far_h_ref, far_l_ref,
     ediff_out_ref, older_out_ref,
     blocks_ref, cond_ref, xh_ref, xl_ref, block_sems, cond_sems) = refs
    parts = collect((own_hbm, other_hbm), blocks_ref, block_sems)
    conds = collect(conds, cond_ref, cond_sems)
    ediff_out_ref[...] = ediff_ref[...]
    older_out_ref[...] = older_ref[...]
    for copy in parts:
        copy.wait()
    for i, step in enumerate(EARLY + LATE):
        for z in range(NZ):
            chip = chip_at(where_ref, step, z)
            a, b = (
                block_of(where_ref, blocks_ref, 2 * chip + core)[:, -WIDTH:] for core in range(2)
            )
            place_pair(a, b, i * NZ + z, xh_ref, xl_ref)
    points = vh_ref.shape[1]
    rows = [
        block_of(where_ref, blocks_ref, 2 * q + core)[:, :points] for q in SENT for core in range(2)
    ]
    whole = jnp.concatenate(rows, axis=0)
    hi, lo = split(whole)
    vh_ref[...] = hi
    vl_ref[...] = lo
    hi, lo = split(whole.T)
    th_ref[...] = hi
    tl_ref[...] = lo
    far_h_ref[...] = xh_ref[:, len(EARLY) * NZ * WIDTH :]
    far_l_ref[...] = xl_ref[:, len(EARLY) * NZ * WIDTH :]
    total = jnp.zeros_like(part_ref)
    for i, step in enumerate(EARLY):
        conds[i].wait()
        ch, cl = split_rows(where_ref, step, cond_ref[i], ch_ref, cl_ref)
        cols = slice(i * NZ * WIDTH, (i + 1) * NZ * WIDTH)
        xh, xl = xh_ref[:, cols], xl_ref[:, cols]
        total += dot(xh, ch) + (dot(xh, cl) + dot(xl, ch))
    part_ref[...] = total


def late_kernel(
    where_ref, part_ref, far_h_ref, far_l_ref, upper_ref, lower_ref, ch_in_ref, cl_in_ref,
    pair_ref, ch_ref, cl_ref,
):
    del ch_in_ref, cl_in_ref
    block = jnp.concatenate([upper_ref[...], lower_ref[...]], axis=0)
    ch, cl = split_rows(where_ref, LATE[0], block, ch_ref, cl_ref)
    xh, xl = far_h_ref[...], far_l_ref[...]
    pair = part_ref[...] + (dot(xh, ch) + (dot(xh, cl) + dot(xl, ch)))
    pair_ref[...] = jnp.broadcast_to(pair[None], pair_ref.shape)


def multiply_pair(xh_ref, xl_ref, ch_ref, cl_ref, pair_ref):
    ch, cl = ch_ref[...], cl_ref[...]
    pair = dot(xh_ref[...], ch) + (dot(xh_ref[...], cl) + dot(xl_ref[...], ch))
    pair_ref[...] = jnp.broadcast_to(pair[None], pair_ref.shape)


def pair_kernel(gathered_ref, ch_ref, cl_ref, pair_ref, xh_ref, xl_ref):
    pair = jnp.zeros(pair_ref.shape[1:], F32)
    for z in range(NZ):
        for q in range(z * NX, (z + 1) * NX):
            a, b = gathered_ref[sent_at(2 * q)], gathered_ref[sent_at(2 * q + 1)]
            place_pair(a, b, q, xh_ref, xl_ref)
        at = slice(z * NX * WIDTH, (z + 1) * NX * WIDTH)
        xh, xl, ch, cl = xh_ref[:, at], xl_ref[:, at], ch_ref[at, :], cl_ref[at, :]
        pair += dot(xh, ch) + (dot(xh, cl) + dot(xl, ch))
    pair_ref[...] = jnp.broadcast_to(pair[None], pair_ref.shape)


def screen_kernel(pair_ref, screened_ref, vh_ref, vl_ref, th_ref, tl_ref, back_ref):
    ph, pl_ = split(pair_ref[...])
    half = th_ref.shape[0] // 2
    parts = []
    for at in (slice(0, half), slice(half, 2 * half)):
        th, tl = th_ref[at, :], tl_ref[at, :]
        mixed = dot(th, ph) + (dot(th, pl_) + dot(tl, ph))
        parts.append(split(mixed * screened_ref[at, :]))
    wh, wl = (jnp.concatenate(p, axis=0) for p in zip(*parts))
    back_ref[...] = dot(vh_ref[...], wh) + (dot(vh_ref[...], wl) + dot(vl_ref[...], wh))


def direct_kernel(terms_ref, ch_ref, cl_ref, out_ref):
    bh, bl = split(jnp.sum(terms_ref[...], axis=0))
    ch, cl = ch_ref[...], cl_ref[...]
    direct = dot_nt(bh, ch) + (dot_nt(bl, ch) + dot_nt(bh, cl))
    half, width = out_ref.shape[1:]
    left = lax.broadcasted_iota(jnp.int32, (half, width), 1) < width // 2
    for q in range(NX * NZ):
        upper = direct[:half, q * width : (q + 1) * width]
        lower = direct[half:, q * width : (q + 1) * width]
        out_ref[sent_at(2 * q)] = jnp.where(left, upper, pltpu.roll(lower, width // 2, 1))
        out_ref[sent_at(2 * q + 1)] = jnp.where(left, pltpu.roll(upper, width // 2, 1), lower)


def scaled(terms_ref, vec, ediff_ref):
    hamil = ediff_ref[...] * vec - jnp.sum(terms_ref[...], axis=0)
    return (hamil - CENTER * vec) / HALF_WIDTH


def first_kernel(terms_ref, vec_ref, ediff_ref, new_ref, copies_ref):
    new = scaled(terms_ref, vec_ref[...], ediff_ref)
    new_ref[...] = new
    copies_ref[...] = jnp.broadcast_to(new[None], copies_ref.shape)


def last_kernel(terms_ref, vec_ref, older_ref, ediff_ref, out_ref):
    new = 2.0 * scaled(terms_ref, vec_ref[...], ediff_ref) - older_ref[...]
    half, width = new.shape
    out_ref[:half, :] = new[:, : width // 2]
    out_ref[half:, :] = new[:, width // 2 :]


def call(kernel, out_shapes, operands, scratch=(), far=(), aliases=None):
    shapes = [jax.ShapeDtypeStruct(s, d) for s, d in out_shapes]
    spaces = [pltpu.SMEM if a.dtype == jnp.int32 else pltpu.VMEM for a in operands]
    for i in far:
        spaces[i] = pltpu.HBM
        operands[i] = pltpu.with_memory_space_constraint(operands[i], pltpu.HBM)
    return pl.pallas_call(
        kernel,
        out_shape=shapes if len(shapes) > 1 else shapes[0],
        scratch_shapes=list(scratch),
        in_specs=[pl.BlockSpec(memory_space=space) for space in spaces],
        input_output_aliases=aliases or {},
        compiler_params=PARAMS,
    )(*operands)


def per_device(vectors, eval_energy, cond_energy, val_orbitals, cond_orbitals, screened):
    _, rows, cols = vectors.shape
    pts, val = lax.axis_size(PTS), lax.axis_size(VAL)
    depth_c, points_c = cond_orbitals.shape
    depth_v, points_v = val_orbitals.shape
    nv, nc = rows * val, cols * pts
    half, width = rows // 2, cols * 2

    zh, core = lax.axis_index("zh"), lax.axis_index("core")
    p = jnp.arange(pts)
    chip = jnp.arange(val)
    where = [lax.axis_index(X)[None], (p & 1) ^ core, chip % NY * 2 + (chip // NY ^ zh)]
    where = jnp.concatenate(where).astype(jnp.int32)
    older = packed(vectors[0])
    ediff = packed(cond_energy[None, :] - eval_energy[:, None])

    mine = copied(cond_orbitals, Z).reshape(-1, points_c)
    parcel = jnp.concatenate([val_orbitals, older], axis=1)
    parcel = jnp.concatenate([parcel, shifted(parcel, "zh", 1)], axis=0)
    own = copied(parcel, "y").reshape(-1, depth_v, points_v + width)
    other = shifted(own, "core", 1)
    left, right = shifted(mine, X, 1), shifted(mine, X, -1)
    part = mine.shape[0] // 2
    upper, lower = shifted(left[:part], X, 1), shifted(right[part:], X, -1)

    newer = older
    scratch = [pltpu.VMEM((rows, nc), BF16)] * 2
    far = nc // NX
    conds = [((nc, points_c), BF16)] * 2
    vh, vl, th, tl, ch, cl, pair, far_h, far_l, ediff, older = call(
        early_kernel,
        [((nv, points_v), BF16)] * 2
        + [((points_v, nv), BF16)] * 2
        + conds
        + [((rows, points_c), F32)]
        + [((rows, far), BF16)] * 2
        + [((half, width), F32)] * 2,
        [where, ediff, older, own, other, mine, left, right],
        [pltpu.VMEM((2, *own.shape), F32), pltpu.VMEM((len(EARLY), *mine.shape), F32)]
        + scratch
        + [pltpu.SemaphoreType.DMA((2,)), pltpu.SemaphoreType.DMA((len(EARLY),))],
        far=range(3, 8),
    )
    pair, ch, cl = call(
        late_kernel,
        [((val, rows, points_c), F32)] + conds,
        [where, pair, far_h, far_l, upper, lower, ch, cl],
        aliases={6: 1, 7: 2},
    )
    for step in range(ITERS):
        if step > 0:
            pair = call(
                pair_kernel,
                [((val, rows, points_c), F32)],
                [exchange(copies, SWEEP), ch, cl],
                scratch,
            )
        pair_all = exchange(pair, SEND).reshape(nv, points_c)
        back = call(
            screen_kernel, [((nv, points_c), F32)], [pair_all, screened, vh, vl, th, tl]
        )
        back = exchange(back.reshape(val, rows, points_c), SEND)
        direct = call(direct_kernel, [((pts, half, width), F32)], [back, ch, cl])
        direct = exchange(direct, SWEEP)
        if step < ITERS - 1:
            newer, copies = call(
                first_kernel,
                [((half, width), F32), ((pts, half, width), F32)],
                [direct, older, ediff],
            )
    out = call(last_kernel, [((rows, cols), F32)], [direct, newer, older, ediff])
    return out[None]


def solution(mesh):
    torus = Mesh(mesh.devices.reshape(2, 8, 2, 2, 2, 2, 2), PTS + Z + X)
    placed = (P(None, VAL, PTS), P(VAL), P(PTS), P(PTS, VAL), P(VAL, PTS), P(VAL, PTS))
    return jax.shard_map(
        per_device, mesh=torus, in_specs=placed, out_specs=P(None, VAL, PTS), check_vma=False
    )
```
